128 devices in a mesh: section: 8 (over x_hi, y), tensor: 16 (over x_lo, z, core).
Axes of the slice: x: 4 (x_hi: 2, x_lo: 2; x = x_hi * 2 + x_lo), y: 4, z: 4, core: 2. Of those that a mesh axis runs over, the one named last changes fastest.
Arguments:
- hidden: bfloat16 [2, 192, 8192], P(None, 'section', 'tensor'), may hold values from -16 to 16
- policy_head: bfloat16 [98304, 8192], P(('section', 'tensor')), may hold values from -1 to 1
- frozen_head: bfloat16 [98304, 8192], P(('section', 'tensor')), may hold values from -1 to 1
- targets: int32 [2, 192], replicated, may hold values from 0 to 98303
- loss_mask: int32 [2, 192], replicated, may hold values 0 or 1
Outputs:
- hidden_grad: bfloat16 [2, 192, 8192], P(None, 'section', 'tensor')
- token_loss: float32 [2, 192], P(None, 'section')
The draws below stay inside these ranges and needn't reach their ends.
All inputs are finite; a program needn't handle non-finite values.
Results may differ from the reference program's by a relative error of at most 0.0036.
Values may be sent and summed in bfloat16 or wider, within the bound.
A program may use at most 128 MiB of HBM per device.

```python
import math
import jax
import jax.numpy as jnp
import numpy as np

D = 8192
V = 98304
MB = 2
TOK_MB = 192


def head_rows(key, rows):

    def one_row(row):
        noise = jnp.clip(jax.random.normal(jax.random.fold_in(key, row), (D,), jnp.float32), -5.0, 5.0)
        return jnp.clip(noise * (3.0 / math.sqrt(D)), -1.0, 1.0)
    return jax.vmap(one_row)(rows)


def draw_policy_head(key, part):
    rows = jnp.arange(V, dtype=jnp.int32)
    values = head_rows(key, rows)
    return values.astype(jnp.bfloat16)


def draw_frozen_head(key, part):
    base_key = key
    key = jax.random.fold_in(key, 2)
    rows = jnp.arange(V, dtype=jnp.int32)
    values = 0.6 * head_rows(base_key, rows) + 0.8 * head_rows(key, rows)
    return jnp.clip(values, -1.0, 1.0).astype(jnp.bfloat16)


def draw_hidden(key, part):
    key = jax.random.fold_in(key, 3)
    values = jnp.clip(jax.random.normal(key, (MB, TOK_MB, D), jnp.float32), -5.0, 5.0)
    return values.astype(jnp.bfloat16)


def touch_ends(values, key, least, high):
    longest = values.shape.index(max(values.shape))
    spots = []
    for shift in (0, 1):
        where = [jax.random.randint(jax.random.fold_in(key, axis), (), 0, length) for axis, length in enumerate(values.shape)]
        where[longest] = (where[longest] + shift) % values.shape[longest]
        spots.append(tuple(where))
    return values.at[spots[0]].set(least).at[spots[1]].set(high)


def ranked_wide(key, shape, count, slope):
    portions = [min(1 << octave, count + 1 - (1 << octave)) * (1 << 20) // math.isqrt((1 << octave) ** slope) + 1 for octave in range((count + 1).bit_length()) if 1 << octave <= count]
    deviation = 1 + sum(portions) // (1 << 30)
    listing = np.cumsum(np.array([max(1, weight // deviation) for weight in portions]))
    pick = jax.random.randint(jax.random.fold_in(key, 1), shape, 0, int(listing[len(portions) - 1]))
    start = jnp.left_shift(1, jnp.searchsorted(jnp.asarray(listing, jnp.int32), pick, side="right").astype(jnp.int32))
    rank = start - 1 + jax.random.randint(jax.random.fold_in(key, 4), shape, 0, 1 << 30) % jnp.minimum(start, count + 1 - start)
    return jax.random.permutation(jax.random.fold_in(key, 2), count)[rank].astype(jnp.int32)


def setup_inputs(seed: int = 0) -> dict:
    key_list = jax.random.split(jax.random.key(seed), 6)
    return {
        "hidden": draw_hidden(jax.random.fold_in(key_list[5], 71), 0),
        "policy_head": draw_policy_head(jax.random.fold_in(key_list[5], 71), 0),
        "frozen_head": draw_frozen_head(jax.random.fold_in(key_list[5], 71), 0),
        "targets": touch_ends(ranked_wide(key_list[3], (MB, TOK_MB), V, 2), jax.random.fold_in(key_list[3], 3), 0, V - 1).astype(jnp.int32),
        "loss_mask": touch_ends((jax.random.randint(key_list[4], (MB, TOK_MB), 0, 4) < 3).astype(jnp.int32), jax.random.fold_in(key_list[4], 1), 0, 1),
    }


divergence_weight = 0.1
gradient_scale = 32.0


def one_batch(hidden_rows, policy_head, frozen_head, labels, valid):
    policy_logits = jnp.dot(hidden_rows, policy_head.T, preferred_element_type=jnp.float32)
    frozen_logits = jnp.dot(hidden_rows, frozen_head.T, preferred_element_type=jnp.float32)
    gap = policy_logits - frozen_logits
    top_policy = jnp.max(policy_logits, axis=1)
    shifted = jnp.exp(policy_logits - top_policy[:, None])
    total_policy = jnp.sum(shifted, axis=1)
    mean_gap = jnp.sum(shifted * gap, axis=1) / total_policy
    top_frozen = jnp.max(frozen_logits, axis=1)
    total_frozen = jnp.sum(jnp.exp(frozen_logits - top_frozen[:, None]), axis=1)
    log_policy = top_policy + jnp.log(total_policy)
    log_frozen = top_frozen + jnp.log(total_frozen)
    columns = jnp.arange(V, dtype=jnp.int32)
    chosen = labels[:, None] == columns[None, :]
    target_logit = jnp.sum(jnp.where(chosen, policy_logits, 0.0), axis=1)
    weight = valid.astype(jnp.float32)
    token_loss = weight * (log_policy - target_logit + divergence_weight * (mean_gap - log_policy + log_frozen))
    probs = jnp.exp(policy_logits - log_policy[:, None])
    logit_grad = gradient_scale * weight[:, None] * (probs - chosen.astype(jnp.float32) + divergence_weight * probs * (gap - mean_gap[:, None]))
    logit_grad = logit_grad.astype(jnp.bfloat16)
    hidden_grad = jnp.dot(logit_grad, policy_head, preferred_element_type=jnp.float32).astype(jnp.bfloat16)
    return hidden_grad, token_loss


def reference(hidden, policy_head, frozen_head, targets, loss_mask):
    grads_out = []
    losses_out = []
    for micro_batch in range(MB):
        grad_rows, loss_rows = one_batch(hidden[micro_batch], policy_head, frozen_head, targets[micro_batch], loss_mask[micro_batch])
        grads_out.append(grad_rows)
        losses_out.append(loss_rows)
    return jnp.stack(grads_out), jnp.stack(losses_out)
```

```python
import functools

import jax
import jax.numpy as jnp
from jax import lax
from jax.experimental import pallas as pl
from jax.experimental.pallas import tpu as pltpu
from jax.sharding import PartitionSpec as P

MESH = pl.DeviceIdType.MESH
divergence_weight = 0.1
gradient_scale = 32.0
N = 4


def device(x, y, z, core):
    return {"section": (x // 2) * N + y, "tensor": (x % 2) * (2 * N) + z * 2 + core}


def wrap(a):
    return lax.rem(a, N)


def kernel(feat, vocab, hidden, policy, frozen, targets, loss_mask, grad_out, loss_out,
           heads_p, heads_f, rows_all, acc_p, acc_f, logit_grad,
           ints, target_col, mask_col, mask_row, lse_col, gap_col, stat_col, stat_loc, stat_twin, stat_chip, stat_in, stat_fin,
           part_own, part_send, part_in, part_half,
           in1a, in1b, in1c, mid_a, mid_b, mid_c, send2a, send2b, send2c, in2a, in2b, in2c, in3,
           head_sem, g1s, g1r, g2s, g2r, g3s, g3r, gts, gtr,
           ss, sr, as_, ar, fs, fr,
           ts, tr, r1as, r1ar, r1s, r1r, r2as, r2ar, r2s, r2r, r3s, r3r):
    f32, bf16 = jnp.float32, jnp.bfloat16
    section, tensor = lax.axis_index("section"), lax.axis_index("tensor")
    x_hi, y = section // N, wrap(section)
    x_lo, z, core = tensor // (2 * N), wrap(tensor // 2), lax.rem(tensor, 2)
    x = x_hi * 2 + x_lo
    twin = 1 - core
    here = {"x": x, "y": y, "z": z}
    wide = 2 * feat

    def peer(axis, d):
        at = dict(here)
        at[axis] = wrap(at[axis] + d)
        return device(at["x"], at["y"], at["z"], core)

    twin_id = device(x, y, z, twin)

    def lanes(start, size, unit):
        return pl.ds(pl.multiple_of(start, unit), size)

    def remote(src, dst, send, recv, to):
        return pltpu.make_async_remote_copy(src, dst, send, recv, device_id=to, device_id_type=MESH)

    def head_copy(head, held, which, k, zz):
        for cc in range(2):
            for lo in range(2):
                pltpu.make_async_copy(
                    head.at[:, lanes((lo * 2 * N + zz * 2 + cc) * feat, feat, feat)],
                    held.at[zz, :, pl.ds((cc * 2 + lo) * feat, feat)],
                    head_sem.at[which, k],
                ).start()

    def head_wait(head, held, which, k, zz):
        pltpu.make_async_copy(head.at[:, pl.ds(0, 4 * feat)], held.at[zz], head_sem.at[which, k]).wait()

    def turn(k):
        return k ^ (k // 2)

    @pl.loop(0, N)
    def _(k):
        zz = wrap(z + turn(k))
        head_copy(policy, heads_p, 0, k, zz)
        head_copy(frozen, heads_f, 1, k, zz)

    barrier = pltpu.get_barrier_semaphore()
    for axis in "xyz":
        for d in range(1, N):
            pl.semaphore_signal(barrier, inc=1, device_id=peer(axis, d), device_id_type=MESH)
    pl.semaphore_signal(barrier, inc=1, device_id=twin_id, device_id_type=MESH)

    own = hidden[...].astype(f32).reshape(48, feat)
    own_cols = core * wide + x_lo * feat
    row_of = (y * 32 + x_hi * 16, 128 + x_hi * 64 + y * 16, 256 + y * 32 + x_hi * 16)
    for g in range(3):
        rows_all[z, lanes(row_of[g], 16, 16), lanes(own_cols, feat, feat)] = own[g * 16 : g * 16 + 16].astype(bf16)
    pl.semaphore_wait(barrier, 3 * (N - 1) + 1)

    axes = (("x", "y", "z"), ("y", "z", "x"), ("x", "z", "y"))

    def piece1(g, at):
        p = {**here, **at}
        hi, lo = p["x"] // 2, lax.rem(p["x"], 2)
        row = 128 + hi * 64 + p["y"] * 16 if g == 1 else g * 128 + p["y"] * 32 + hi * 16
        return rows_all.at[p["z"], lanes(row, 16, 16), lanes(core * wide + lo * feat, feat, feat)]

    def piece2(g, at):
        p = {**here, **at}
        hi, lo = p["x"] // 2, lax.rem(p["x"], 2)
        if g == 1:
            return rows_all.at[p["z"], lanes(128 + hi * 64, 64, 64), lanes(core * wide + lo * feat, feat, feat)]
        return rows_all.at[p["z"], lanes(g * 128 + p["y"] * 32, 32, 32), lanes(core * wide, wide, wide)]

    def back(axis, d):
        return wrap(here[axis] + N - d)

    def stage1(g, d):
        return remote(piece1(g, {}), piece1(g, {}), g1s.at[g, d - 1], g1r.at[g, d - 1], peer(axes[g][0], d))

    def stage1_in(g, d):
        ref = piece1(g, {axes[g][0]: back(axes[g][0], d)})
        return remote(ref, ref, g1s.at[g, d - 1], g1r.at[g, d - 1], peer(axes[g][0], d))

    def stage2(g, d):
        return remote(piece2(g, {}), piece2(g, {}), g2s.at[g, d - 1], g2r.at[g, d - 1], peer(axes[g][1], d))

    def stage2_in(g, d):
        ref = piece2(g, {axes[g][1]: back(axes[g][1], d)})
        return remote(ref, ref, g2s.at[g, d - 1], g2r.at[g, d - 1], peer(axes[g][1], d))

    def stage3(g, d, q):
        ref = piece2(g, {axes[g][1]: wrap(here[axes[g][1]] + q)})
        return remote(ref, ref, g3s.at[g, d - 1, q], g3r.at[g, d - 1, q], peer(axes[g][2], d))

    def stage3_in(g, d, q):
        ref = piece2(g, {axes[g][1]: wrap(here[axes[g][1]] + q), axes[g][2]: back(axes[g][2], d)})
        return remote(ref, ref, g3s.at[g, d - 1, q], g3r.at[g, d - 1, q], peer(axes[g][2], d))

    near_first = (1, 3, 2)
    for g in range(3):
        for d in near_first:
            stage1(g, d).start()

    acc_p[...] = jnp.zeros_like(acc_p)
    acc_f[...] = jnp.zeros_like(acc_f)
    ints[...] = jnp.zeros_like(ints)
    ints[0:2, 0:192] = targets[...].astype(f32)
    ints[2:4, 0:192] = loss_mask[...].astype(f32)
    for base, col in ((0, target_col), (2, mask_col)):
        for mb in range(2):
            for half in range(2):
                line = ints[base + mb : base + mb + 1, half * 128 : half * 128 + 128]
                upright = jnp.broadcast_to(line, (128, 128)).T
                for q in range(16 if half == 0 else 8):
                    chunk = half * 16 + q
                    s, h = chunk // 3, chunk % 3
                    flat = mb * 24 + h * 8
                    g, j = flat // 16, flat % 16
                    hi, yy = s // N, s % N
                    row = 128 + hi * 64 + yy * 16 if g == 1 else g * 128 + yy * 32 + hi * 16
                    col[row + j : row + j + 8, :] = upright[q * 8 : q * 8 + 8, :]
    for j in range(3):
        mask_row[j : j + 1, :] = mask_col[j * 128 : j * 128 + 128, :].T[0:1, :]

    for g in range(3):
        for d in near_first:
            stage1_in(g, d).wait_recv()
        for d in near_first:
            stage2(g, d).start()
            stage3(g, d, 0).start()
    for q in near_first:
        for g in (1, 2, 0):
            stage2_in(g, N - q).wait_recv()
            for d in near_first:
                stage3(g, d, q).start()

    contract = (((1,), (1,)), ((), ()))

    def twin_copy(r):
        zz = wrap(z + r)
        ref = rows_all.at[zz, :, lanes(core * wide, wide, wide)]
        return remote(ref, ref, gts.at[r], gtr.at[r], twin_id)

    def twin_in(r):
        zz = wrap(z + r)
        ref = rows_all.at[zz, :, lanes(twin * wide, wide, wide)]
        return remote(ref, ref, gts.at[r], gtr.at[r], twin_id)

    @pl.loop(0, N)
    def _(k):
        r = turn(k)
        zz = wrap(z + r)
        for d in near_first:
            stage3_in(1, d, r).wait_recv()
            stage3_in(2, d, r).wait_recv()

        @pl.when(k > 0)
        def _():
            d = N - r
            for q in range(N):
                stage3_in(0, d, q).wait_recv()

        twin_copy(r).start()
        head_wait(policy, heads_p, 0, k, zz)
        head_wait(frozen, heads_f, 1, k, zz)
        twin_in(r).wait_recv()
        acc_p[...] += lax.dot_general(rows_all[zz], heads_p[zz], contract, preferred_element_type=f32)
        acc_f[...] += lax.dot_general(rows_all[zz], heads_f[zz], contract, preferred_element_type=f32)

    shard = section * (4 * N) + tensor
    first = (shard * vocab).astype(f32)
    block = 32
    lane = lax.broadcasted_iota(jnp.int32, (block, 128), 1)

    def picked(rows, v):
        return (lane + v * 128).astype(f32) == target_col[rows, :] - first

    @pl.loop(0, 384 // block)
    def _(i):
        rows = pl.ds(pl.multiple_of(i * block, block), block)
        tiles = vocab // 128
        lp = [acc_p[rows, v * 128 : v * 128 + 128] for v in range(tiles)]
        lf = [acc_f[rows, v * 128 : v * 128 + 128] for v in range(tiles)]
        top_p = jnp.max(functools.reduce(jnp.maximum, lp), axis=1, keepdims=True)
        top_f = jnp.max(functools.reduce(jnp.maximum, lf), axis=1, keepdims=True)
        ep = [jnp.exp(a - top_p) for a in lp]
        sum_p = jnp.sum(functools.reduce(jnp.add, ep), axis=1, keepdims=True)
        gaps = jnp.sum(functools.reduce(jnp.add, [e * (a - b) for e, a, b in zip(ep, lp, lf)]), axis=1, keepdims=True)
        sum_f = jnp.sum(functools.reduce(jnp.add, [jnp.exp(b - top_f) for b in lf]), axis=1, keepdims=True)
        hit = jnp.sum(
            functools.reduce(jnp.add, [jnp.where(picked(rows, v), lp[v], 0.0) for v in range(tiles)]),
            axis=1, keepdims=True,
        )
        stat_col[rows, :] = jnp.where(
            lane == 0, top_p + jnp.log(sum_p),
            jnp.where(lane == 1, gaps / sum_p, jnp.where(lane == 2, top_f + jnp.log(sum_f), hit)),
        )

    stat_loc[...] = jnp.zeros_like(stat_loc)
    for j in range(3):
        upright = stat_col[j * 128 : j * 128 + 128, :].T
        for s in range(4):
            stat_loc[s // 2, (s % 2) * 3 + j : (s % 2) * 3 + j + 1, :] = upright[s : s + 1, :]

    first_core = core == 0

    def merge(tiles):
        top = functools.reduce(jnp.maximum, tiles)
        scaled = [jnp.exp(t - top) for t in tiles]
        total = functools.reduce(jnp.add, scaled)
        moved = [jnp.where(first_core, jnp.roll(s, 3, axis=0), 1.0) for s in scaled]
        weighted = functools.reduce(jnp.add, [m * t for m, t in zip(moved, tiles)])
        below = jnp.where(first_core, jnp.roll(total, 3, axis=0), 1.0)
        sub = lax.broadcasted_iota(jnp.int32, (8, 128), 0)
        return jnp.where(sub < 3, top + jnp.log(total), weighted / below)

    to_twin = remote(stat_loc.at[twin], stat_twin, ss.at[0], sr.at[0], twin_id)
    to_twin.start()
    to_twin.wait_recv()
    stat_chip[...] = merge([stat_loc[core], stat_twin[...]])

    def stat_copy(k):
        to = device(wrap(x + k // 16), wrap(y + k // 4), wrap(z + k), core)
        return remote(stat_chip, stat_in.at[k - 1], as_, ar, to)

    @pl.loop(1, 64)
    def _(k):
        stat_copy(k).start()

    pltpu.make_async_copy(stat_in, stat_in, ar).wait()
    stat_fin[core] = merge([stat_chip[...]] + [stat_in[k] for k in range(63)])
    fin = remote(stat_fin.at[core], stat_fin.at[core], fs.at[0], fr.at[0], twin_id)
    fin.start()
    remote(stat_fin.at[twin], stat_fin.at[twin], fs.at[0], fr.at[0], twin_id).wait_recv()

    for j in range(3):
        rows = slice(j * 128, j * 128 + 128)
        lse_col[rows, :] = jnp.broadcast_to(stat_fin[0, j : j + 1, :], (128, 128)).T
        gap_col[rows, :] = jnp.broadcast_to(stat_fin[0, 3 + j : 4 + j, :], (128, 128)).T

    @pl.loop(0, 384 // block)
    def _(i):
        rows = pl.ds(pl.multiple_of(i * block, block), block)
        lse, mean_gap, weight = lse_col[rows, :], gap_col[rows, :], gradient_scale * mask_col[rows, :]
        for v in range(vocab // 128):
            at = slice(v * 128, v * 128 + 128)
            lp, lf = acc_p[rows, at], acc_f[rows, at]
            probs = jnp.exp(lp - lse)
            hot = jnp.where(picked(rows, v), 1.0, 0.0)
            g = weight * (probs - hot + divergence_weight * probs * (lp - lf - mean_gap))
            logit_grad[rows, at] = g.astype(bf16)

    def turn_back(k):
        return turn(k) ^ 2

    def part_copy(k):
        slot = lax.rem(k, 2)
        return remote(part_send.at[slot], part_in.at[k], ts.at[slot], tr.at[k], twin_id)

    def back1a(k):
        r = turn_back(k)
        return remote(part_half.at[k, pl.ds(0, 128)], in1a.at[r - 1], r1as.at[r - 1], r1ar.at[r - 1], peer("z", r))

    def back1b(k, d):
        to = wrap(x + d)
        src = part_half.at[k, lanes(128 + (to // 2) * 64, 64, 64), lanes(lax.rem(to, 2) * feat, feat, feat)]
        return remote(src, in1b.at[k, d - 1], r1s.at[0, k, d - 1], r1r.at[0, k, d - 1], peer("x", d))

    def back1c(k, d):
        src = part_half.at[k, lanes(256 + wrap(y + d) * 32, 32, 32)]
        return remote(src, in1c.at[k, d - 1], r1s.at[1, k, d - 1], r1r.at[1, k, d - 1], peer("y", d))

    @pl.loop(0, N)
    def _(k):
        r = turn_back(k)
        zz = wrap(z + r)
        slot = lax.rem(k, 2)

        @pl.when(k >= 2)
        def _():
            part_copy(k).wait_send()

        part_send[slot] = jnp.dot(
            logit_grad[...], heads_p[zz, :, lanes(twin * wide, wide, wide)], preferred_element_type=f32
        )
        part_copy(k).start()
        part_own[k] = jnp.dot(
            logit_grad[...], heads_p[zz, :, lanes(core * wide, wide, wide)], preferred_element_type=f32
        )
        part_copy(k).wait_recv()

        @pl.loop(0, 384 // 16)
        def _(i):
            rows = pl.ds(pl.multiple_of(i * 16, 16), 16)
            total = part_own[k, rows, :] + part_in[k, rows, :]
            part_own[k, rows, :] = total
            part_half[k, rows, :] = total.astype(bf16)

        for d in near_first:
            back1b(k, d).start()
            back1c(k, d).start()

        @pl.when(k < N - 1)
        def _():
            back1a(k).start()

    def back2a(d):
        src = send2a.at[lanes(wrap(y + d) * 32, 32, 32)]
        return remote(src, in2a.at[d - 1], r2as.at[d - 1], r2ar.at[d - 1], peer("y", d))

    def back2b(k):
        r = turn_back(k)
        return remote(send2b.at[r - 1], in2b.at[r - 1], r2s.at[0, r - 1], r2r.at[0, r - 1], peer("z", r))

    def back2c(k):
        r = turn_back(k)
        return remote(send2c.at[r - 1], in2c.at[r - 1], r2s.at[1, r - 1], r2r.at[1, r - 1], peer("z", r))

    @pl.loop(0, N)
    def _(k):
        r = turn_back(k)
        for d in near_first:
            back1b(k, d).wait_recv()
            back1c(k, d).wait_recv()
        total_b = part_own[k, lanes(128 + x_hi * 64, 64, 64), lanes(x_lo * feat, feat, feat)]
        total_c = part_own[k, lanes(256 + y * 32, 32, 32), :]
        for d in range(3):
            total_b += in1b[k, d].astype(f32)
            total_c += in1c[k, d].astype(f32)

        @pl.when(k < N - 1)
        def _():
            send2b[r - 1] = total_b.astype(bf16)
            send2c[r - 1] = total_c.astype(bf16)
            back2b(k).start()
            back2c(k).start()

        @pl.when(k == N - 1)
        def _():
            mid_b[...] = total_b
            mid_c[...] = total_c

    for d in near_first:
        back1a_in = remote(in1a.at[d - 1], in1a.at[d - 1], r1as.at[d - 1], r1ar.at[d - 1], peer("z", d))
        back1a_in.wait_recv()

    @pl.loop(0, N)
    def _(i):
        rows = pl.ds(pl.multiple_of(i * 32, 32), 32)
        total = part_own[N - 1, rows, :]
        for d in range(3):
            total += in1a[d, rows, :].astype(f32)
        send2a[rows, :] = total.astype(bf16)

        @pl.when(i == y)
        def _():
            mid_a[...] = total

    for d in near_first:
        back2a(d).start()

    def back3(g, d):
        if g == 1:
            src = mid_b.at[lanes(wrap(y + d) * 16, 16, 16)]
            return remote(src, in3.at[g, d - 1], r3s.at[g, d - 1], r3r.at[g, d - 1], peer("y", d))
        to = wrap(x + d)
        src = (mid_a if g == 0 else mid_c).at[lanes((to // 2) * 16, 16, 16), lanes(lax.rem(to, 2) * feat, feat, feat)]
        return remote(src, in3.at[g, d - 1], r3s.at[g, d - 1], r3r.at[g, d - 1], peer("x", d))

    for g, mid, inbox in ((1, mid_b, in2b), (2, mid_c, in2c), (0, mid_a, in2a)):
        for d in near_first:
            if g == 0:
                remote(in2a.at[d - 1], in2a.at[d - 1], r2as.at[d - 1], r2ar.at[d - 1], peer("y", d)).wait_recv()
            else:
                remote(inbox.at[d - 1], inbox.at[d - 1], r2s.at[g - 1, d - 1], r2r.at[g - 1, d - 1], peer("z", d)).wait_recv()
        mid[...] += inbox[0].astype(f32) + inbox[1].astype(f32) + inbox[2].astype(f32)
        for d in near_first:
            back3(g, d).start()

    sub8 = lax.broadcasted_iota(jnp.int32, (8, 128), 0)
    lane8 = lax.broadcasted_iota(jnp.int32, (8, 128), 1)
    lse_p, extra = stat_fin[0], stat_fin[1]
    mean_gap8, hit8 = jnp.roll(lse_p, -3, axis=0), jnp.roll(extra, -3, axis=0)
    losses = mask_row[...] * (lse_p - hit8 + divergence_weight * (mean_gap8 - lse_p + extra))
    lined = jnp.zeros((8, 128), f32)
    for g in range(3):
        at = row_of[g] - g * 128
        moved = pltpu.roll(losses, lax.rem(128 - at + g * 16, 128), 1)
        line = jnp.broadcast_to(moved[g : g + 1, :], (8, 128))
        lined = jnp.where((lane8 >= g * 16) & (lane8 < g * 16 + 16), line, lined)
    second = pltpu.roll(lined, 128 - 24, 1)
    loss_out[...] = jnp.where(sub8 == 0, lined, second)[0:2, 0:24]

    done = []
    for g in range(3):
        for d in near_first:
            back3(g, d).wait_recv()
        if g == 1:
            total = mid_b[lanes(y * 16, 16, 16), :]
        else:
            total = (mid_a if g == 0 else mid_c)[lanes(x_hi * 16, 16, 16), lanes(x_lo * feat, feat, feat)]
        done.append(total + in3[g, 0] + in3[g, 1] + in3[g, 2])
    grad_out[...] = jnp.concatenate(done, axis=0).reshape(2, 24, feat).astype(bf16)

    for g in range(3):
        for d in near_first:
            stage1(g, d).wait_send()
            stage2(g, d).wait_send()
            for q in range(N):
                stage3(g, d, q).wait_send()
            back3(g, d).wait_send()
    to_twin.wait_send()
    pltpu.make_async_copy(stat_in, stat_in, as_).wait()
    fin.wait_send()
    for r in range(N):
        twin_copy(r).wait_send()
    part_copy(2).wait_send()
    part_copy(3).wait_send()
    for k in range(N):
        for d in near_first:
            back1b(k, d).wait_send()
            back1c(k, d).wait_send()
        if k < N - 1:
            back1a(k).wait_send()
            back2b(k).wait_send()
            back2c(k).wait_send()
            back2a(k + 1).wait_send()


def body(hidden, policy_head, frozen_head, targets, loss_mask):
    vocab = policy_head.shape[0]
    feat = hidden.shape[2]
    wide = 2 * feat
    f32, bf16 = jnp.float32, jnp.bfloat16
    V, D = pltpu.VMEM, pltpu.SemaphoreType.DMA
    scratch = [
        V((N, vocab, 2 * wide), bf16), V((N, vocab, 2 * wide), bf16), V((N, 384, 2 * wide), bf16),
        V((384, vocab), f32), V((384, vocab), f32), V((384, vocab), bf16),
        V((8, 256), f32), V((384, 128), f32), V((384, 128), f32), V((8, 128), f32), V((384, 128), f32), V((384, 128), f32),
        V((384, 128), f32), V((2, 8, 128), f32), V((8, 128), f32), V((8, 128), f32), V((63, 8, 128), f32), V((2, 8, 128), f32),
        V((N, 384, wide), f32), V((2, 384, wide), f32), V((N, 384, wide), f32), V((N, 384, wide), bf16),
        V((3, 128, wide), bf16), V((N, 3, 64, feat), bf16), V((N, 3, 32, wide), bf16),
        V((32, wide), f32), V((64, feat), f32), V((32, wide), f32),
        V((128, wide), bf16), V((3, 64, feat), bf16), V((3, 32, wide), bf16),
        V((3, 32, wide), bf16), V((3, 64, feat), bf16), V((3, 32, wide), bf16), V((3, 3, 16, feat), f32),
        D((2, N)), D((3, 3)), D((3, 3)), D((3, 3)), D((3, 3)), D((3, 3, N)), D((3, 3, N)), D((N,)), D((N,)),
        D((1,)), D((1,)), D, D, D((1,)), D((1,)),
        D((2,)), D((N,)), D((3,)), D((3,)), D((2, N, 3)), D((2, N, 3)), D((3,)), D((3,)), D((2, 3)), D((2, 3)), D((3, 3)), D((3, 3)),
    ]
    vmem = pl.BlockSpec(memory_space=pltpu.VMEM)
    anywhere = pl.BlockSpec(memory_space=pl.ANY)
    return pl.pallas_call(
        functools.partial(kernel, feat, vocab),
        out_shape=(
            jax.ShapeDtypeStruct(hidden.shape, bf16),
            jax.ShapeDtypeStruct(hidden.shape[:2], f32),
        ),
        in_specs=[vmem, anywhere, anywhere, vmem, vmem],
        out_specs=(vmem, vmem),
        scratch_shapes=scratch,
        compiler_params=pltpu.CompilerParams(
            collective_id=0, has_side_effects=True, vmem_limit_bytes=63 * 2**20
        ),
    )(hidden, policy_head, frozen_head, targets, loss_mask)


def solution(mesh):
    in_specs = (
        P(None, "section", "tensor"),
        P(("section", "tensor"), None),
        P(("section", "tensor"), None),
        P(),
        P(),
    )
    out_specs = (P(None, "section", "tensor"), P(None, "section"))
    return jax.shard_map(body, mesh=mesh, in_specs=in_specs, out_specs=out_specs, check_vma=False)
```

```python
import functools

import jax
import jax.numpy as jnp
from jax import lax
from jax.experimental import pallas as pl
from jax.experimental.pallas import tpu as pltpu
from jax.sharding import PartitionSpec as P

MESH = pl.DeviceIdType.MESH
divergence_weight = 0.1
gradient_scale = 32.0
N = 4


def device(x, y, z, core):
    return {"section": (x // 2) * N + y, "tensor": (x % 2) * (2 * N) + z * 2 + core}


def wrap(a):
    return lax.rem(a, N)


def kernel(feat, vocab, hidden_in, policy, frozen, targets_in, mask_in, grad_out, loss_out,
           heads_p, heads_f, rows_all, acc_p, acc_f, logit_grad,
           ints, target_col, mask_col, mask_row, lse_col, gap_col, stat_col, stat_loc, stat_twin, stat_chip, stat_in, stat_fin,
           part_own, part_send, part_in, part_half,
           in1a, in1b, in1c, mid_a, mid_b, mid_c, send2a, send2b, send2c, in2,
           head_sem, gas, gar, g3s, g3r, gts, gtr,
           ss, sr, as_, ar, fs, fr,
           ts, tr, r1s, r1ar, r1r, r2s, r2r, vouch_sem,
           small_sem, hidden, targets, loss_mask):
    f32, bf16 = jnp.float32, jnp.bfloat16
    section, tensor = lax.axis_index("section"), lax.axis_index("tensor")
    x_hi, y = section // N, wrap(section)
    x_lo, z, core = tensor // (2 * N), wrap(tensor // 2), lax.rem(tensor, 2)
    x = x_hi * 2 + x_lo
    twin = 1 - core
    here = {"x": x, "y": y, "z": z}
    wide = 2 * feat

    def peer(axis, d, axis2="x", d2=0):
        at = dict(here)
        at[axis] = wrap(at[axis] + d)
        at[axis2] = wrap(at[axis2] + d2)
        return device(at["x"], at["y"], at["z"], core)

    twin_id = device(x, y, z, twin)

    def lanes(start, size, unit):
        return pl.ds(pl.multiple_of(start, unit), size)

    def remote(src, dst, send, recv, to):
        return pltpu.make_async_remote_copy(src, dst, send, recv, device_id=to, device_id_type=MESH)

    small = [pltpu.make_async_copy(src, dst, small_sem.at[i])
             for i, (src, dst) in enumerate(((hidden_in, hidden), (targets_in, targets), (mask_in, loss_mask)))]
    for copy in small:
        copy.start()

    def head_copy(head, held, which, k, zz):
        for cc in range(2):
            for lo in range(2):
                pltpu.make_async_copy(
                    head.at[:, lanes((lo * 2 * N + zz * 2 + cc) * feat, feat, feat)],
                    held.at[zz, :, pl.ds((cc * 2 + lo) * feat, feat)],
                    head_sem.at[which, k],
                ).start()

    def head_wait(head, held, which, k, zz):
        pltpu.make_async_copy(head.at[:, pl.ds(0, 4 * feat)], held.at[zz], head_sem.at[which, k]).wait()

    def turn(k):
        return k ^ (k // 2)

    @pl.loop(0, N)
    def _(k):
        zz = wrap(z + turn(k))
        head_copy(policy, heads_p, 0, k, zz)
        head_copy(frozen, heads_f, 1, k, zz)

    barrier = pltpu.get_barrier_semaphore()
    for axis in "xyz":
        for d in range(1, N):
            pl.semaphore_signal(barrier, inc=1, device_id=peer(axis, d), device_id_type=MESH)
    pl.semaphore_signal(barrier, inc=1, device_id=twin_id, device_id_type=MESH)

    small[0].wait()
    own = hidden[...].astype(f32).reshape(48, feat)
    own_cols = core * wide + x_lo * feat
    row_of = (y * 32 + x_hi * 16, 128 + x_hi * 64 + y * 16, 256 + y * 32 + x_hi * 16)
    for g in range(3):
        rows_all[z, lanes(row_of[g], 16, 16), lanes(own_cols, feat, feat)] = own[g * 16 : g * 16 + 16].astype(bf16)
    pl.semaphore_wait(barrier, 3 * (N - 1) + 1)
    for axis in "xy":
        for d in range(1, N):
            pl.semaphore_signal(vouch_sem, inc=1, device_id=peer(axis, d), device_id_type=MESH)

    axes = (("x", "y", "z"), ("y", "z", "x"), ("x", "z", "y"))

    def piece1(g, at):
        p = {**here, **at}
        hi, lo = p["x"] // 2, lax.rem(p["x"], 2)
        row = 128 + hi * 64 + p["y"] * 16 if g == 1 else g * 128 + p["y"] * 32 + hi * 16
        return rows_all.at[p["z"], lanes(row, 16, 16), lanes(core * wide + lo * feat, feat, feat)]

    def piece2(g, at):
        p = {**here, **at}
        hi, lo = p["x"] // 2, lax.rem(p["x"], 2)
        if g == 1:
            return rows_all.at[p["z"], lanes(128 + hi * 64, 64, 64), lanes(core * wide + lo * feat, feat, feat)]
        return rows_all.at[p["z"], lanes(g * 128 + p["y"] * 32, 32, 32), lanes(core * wide, wide, wide)]

    def elements(rows, cols, deep=1):
        return rows_all.at[pl.ds(0, deep), pl.ds(0, rows), pl.ds(0, cols)]

    def await_all(ref, sem):
        pltpu.make_async_copy(ref, ref, sem).wait()

    near_first = (1, 3, 2)

    def block_copy(g, d1, d2):
        ref = piece1(g, {})
        return remote(ref, ref, gas, gar.at[g, (N - d2) % N], peer(axes[g][0], d1, axes[g][1], d2))

    def piece_wait(g, q):
        if q == 0:
            await_all(elements(3 * 16, feat), gar.at[g, 0])
        else:
            await_all(piece2(g, {axes[g][1]: wrap(here[axes[g][1]] + q)}), gar.at[g, q])

    def piece_copy(g, d, q):
        ref = piece2(g, {axes[g][1]: wrap(here[axes[g][1]] + q)})
        return remote(ref, ref, g3s, g3r.at[N - d if g == 0 else q], peer(axes[g][2], d))

    for d in near_first:
        for g in (1, 2, 0):
            block_copy(g, d, 0).start()
    for d in near_first:
        for g in (1, 2, 0):
            block_copy(g, 0, d).start()
    pl.semaphore_wait(vouch_sem, 2 * (N - 1))
    for d2 in near_first:
        for d1 in near_first:
            for g in (1, 2, 0):
                block_copy(g, d1, d2).start()

    acc_p[...] = jnp.zeros_like(acc_p)
    acc_f[...] = jnp.zeros_like(acc_f)
    ints[...] = jnp.zeros_like(ints)
    small[1].wait()
    small[2].wait()
    ints[0:2, 0:192] = targets[...].astype(f32)
    ints[2:4, 0:192] = loss_mask[...].astype(f32)
    for base, col in ((0, target_col), (2, mask_col)):
        for mb in range(2):
            for half in range(2):
                line = ints[base + mb : base + mb + 1, half * 128 : half * 128 + 128]
                upright = jnp.broadcast_to(line, (128, 128)).T
                for q in range(16 if half == 0 else 8):
                    chunk = half * 16 + q
                    s, h = chunk // 3, chunk % 3
                    flat = mb * 24 + h * 8
                    g, j = flat // 16, flat % 16
                    hi, yy = s // N, s % N
                    row = 128 + hi * 64 + yy * 16 if g == 1 else g * 128 + yy * 32 + hi * 16
                    col[row + j : row + j + 8, :] = upright[q * 8 : q * 8 + 8, :]
    for j in range(3):
        mask_row[j : j + 1, :] = mask_col[j * 128 : j * 128 + 128, :].T[0:1, :]

    for q in (0, 1, 3, 2):
        for g in (1, 2, 0):
            piece_wait(g, q)
            if g == 0:
                for d in (1, 3):
                    piece_copy(g, d, q).start()
            elif q != 2:
                for d in near_first:
                    piece_copy(g, d, q).start()

    contract = (((1,), (1,)), ((), ()))

    def twin_copy(r):
        zz = wrap(z + r)
        ref = rows_all.at[zz, :, lanes(core * wide, wide, wide)]
        return remote(ref, ref, gts, gtr.at[r], twin_id)

    def twin_in(r):
        zz = wrap(z + r)
        ref = rows_all.at[zz, :, lanes(twin * wide, wide, wide)]
        return remote(ref, ref, gts, gtr.at[r], twin_id)

    await_all(elements(96, 2 * wide), g3r.at[0])
    twin_copy(0).start()
    for q in near_first:
        piece_copy(0, 2, q).start()
    piece_copy(0, 2, 0).start()
    for g in (1, 2):
        for d in near_first:
            piece_copy(g, d, 2).start()
    twin_in(0).wait_recv()

    @pl.loop(0, N)
    def _(k):
        zz = wrap(z + turn(k))
        head_wait(policy, heads_p, 0, k, zz)
        acc_p[...] += lax.dot_general(rows_all[zz], heads_p[zz], contract, preferred_element_type=f32)

        @pl.when(k < N - 1)
        def _():
            await_all(elements(160, 2 * wide), g3r.at[turn(k + 1)])
            twin_copy(turn(k + 1)).start()

        head_wait(frozen, heads_f, 1, k, zz)
        acc_f[...] += lax.dot_general(rows_all[zz], heads_f[zz], contract, preferred_element_type=f32)

        @pl.when(k < N - 1)
        def _():
            twin_in(turn(k + 1)).wait_recv()

    shard = section * (4 * N) + tensor
    first = (shard * vocab).astype(f32)
    block = 32
    lane = lax.broadcasted_iota(jnp.int32, (block, 128), 1)

    def picked(rows, v):
        return (lane + v * 128).astype(f32) == target_col[rows, :] - first

    @pl.loop(0, 384 // block)
    def _(i):
        rows = pl.ds(pl.multiple_of(i * block, block), block)
        tiles = vocab // 128
        lp = [acc_p[rows, v * 128 : v * 128 + 128] for v in range(tiles)]
        lf = [acc_f[rows, v * 128 : v * 128 + 128] for v in range(tiles)]
        top_p = jnp.max(functools.reduce(jnp.maximum, lp), axis=1, keepdims=True)
        top_f = jnp.max(functools.reduce(jnp.maximum, lf), axis=1, keepdims=True)
        ep = [jnp.exp(a - top_p) for a in lp]
        sum_p = jnp.sum(functools.reduce(jnp.add, ep), axis=1, keepdims=True)
        gaps = jnp.sum(functools.reduce(jnp.add, [e * (a - b) for e, a, b in zip(ep, lp, lf)]), axis=1, keepdims=True)
        sum_f = jnp.sum(functools.reduce(jnp.add, [jnp.exp(b - top_f) for b in lf]), axis=1, keepdims=True)
        hit = jnp.sum(
            functools.reduce(jnp.add, [jnp.where(picked(rows, v), lp[v], 0.0) for v in range(tiles)]),
            axis=1, keepdims=True,
        )
        stat_col[rows, :] = jnp.where(
            lane == 0, top_p + jnp.log(sum_p),
            jnp.where(lane == 1, gaps / sum_p, jnp.where(lane == 2, top_f + jnp.log(sum_f), hit)),
        )

    stat_loc[...] = jnp.zeros_like(stat_loc)
    for j in range(3):
        upright = stat_col[j * 128 : j * 128 + 128, :].T
        for s in range(4):
            stat_loc[s // 2, (s % 2) * 3 + j : (s % 2) * 3 + j + 1, :] = upright[s : s + 1, :]

    first_core = core == 0

    def merge(tiles):
        top = functools.reduce(jnp.maximum, tiles)
        scaled = [jnp.exp(t - top) for t in tiles]
        total = functools.reduce(jnp.add, scaled)
        moved = [jnp.where(first_core, jnp.roll(s, 3, axis=0), 1.0) for s in scaled]
        weighted = functools.reduce(jnp.add, [m * t for m, t in zip(moved, tiles)])
        below = jnp.where(first_core, jnp.roll(total, 3, axis=0), 1.0)
        sub = lax.broadcasted_iota(jnp.int32, (8, 128), 0)
        return jnp.where(sub < 3, top + jnp.log(total), weighted / below)

    to_twin = remote(stat_loc.at[twin], stat_twin, ss.at[0], sr.at[0], twin_id)
    to_twin.start()
    to_twin.wait_recv()
    stat_chip[...] = merge([stat_loc[core], stat_twin[...]])

    def stat_copy(k):
        to = device(wrap(x + k // 16), wrap(y + k // 4), wrap(z + k), core)
        return remote(stat_chip, stat_in.at[k - 1], as_, ar, to)

    def hops(k):
        return sum(min(d, N - d) for d in (k // 16, k // 4 % N, k % N))

    for k in sorted(range(1, 64), key=hops, reverse=True):
        stat_copy(k).start()

    pltpu.make_async_copy(stat_in, stat_in, ar).wait()
    stat_fin[core] = merge([stat_chip[...]] + [stat_in[k] for k in range(63)])
    fin = remote(stat_fin.at[core], stat_fin.at[core], fs.at[0], fr.at[0], twin_id)
    fin.start()
    remote(stat_fin.at[twin], stat_fin.at[twin], fs.at[0], fr.at[0], twin_id).wait_recv()

    for j in range(3):
        rows = slice(j * 128, j * 128 + 128)
        lse_col[rows, :] = jnp.broadcast_to(stat_fin[0, j : j + 1, :], (128, 128)).T
        gap_col[rows, :] = jnp.broadcast_to(stat_fin[0, 3 + j : 4 + j, :], (128, 128)).T

    @pl.loop(0, 384 // block)
    def _(i):
        rows = pl.ds(pl.multiple_of(i * block, block), block)
        lse, mean_gap, weight = lse_col[rows, :], gap_col[rows, :], gradient_scale * mask_col[rows, :]
        for v in range(vocab // 128):
            at = slice(v * 128, v * 128 + 128)
            lp, lf = acc_p[rows, at], acc_f[rows, at]
            probs = jnp.exp(lp - lse)
            hot = jnp.where(picked(rows, v), 1.0, 0.0)
            g = weight * (probs - hot + divergence_weight * probs * (lp - lf - mean_gap))
            logit_grad[rows, at] = g.astype(bf16)

    def turn_back(k):
        return turn(k) ^ 2

    def part_copy(k):
        slot = lax.rem(k, 2)
        return remote(part_send.at[slot], part_in.at[k], ts.at[slot], tr.at[k], twin_id)

    def back1a(k):
        r = turn_back(k)
        return remote(part_half.at[k, pl.ds(0, 128)], in1a.at[r - 1], r1s, r1ar, peer("z", r))

    def back1b(k, d):
        to = wrap(x + d)
        src = part_half.at[k, lanes(128 + (to // 2) * 64, 64, 64), lanes(lax.rem(to, 2) * feat, feat, feat)]
        return remote(src, in1b.at[k, d - 1], r1s, r1r.at[k], peer("x", d))

    def back1c(k, d):
        src = part_half.at[k, lanes(256 + wrap(y + d) * 32, 32, 32)]
        return remote(src, in1c.at[k, d - 1], r1s, r1r.at[k], peer("y", d))

    def part_dot(k, half):
        zz = wrap(z + turn_back(k))
        return jnp.dot(logit_grad[...], heads_p[zz, :, lanes(half * wide, wide, wide)], preferred_element_type=f32)

    part_send[0] = part_dot(0, twin)
    part_copy(0).start()

    @pl.loop(0, N)
    def _(k):
        part_own[k] = part_dot(k, core)

        @pl.when(k < N - 1)
        def _():
            @pl.when(k >= 1)
            def _():
                part_copy(k - 1).wait_send()

            part_send[lax.rem(k + 1, 2)] = part_dot(k + 1, twin)
            part_copy(k + 1).start()

        part_copy(k).wait_recv()

        @pl.loop(0, 384 // 16)
        def _(i):
            rows = pl.ds(pl.multiple_of(i * 16, 16), 16)
            total = part_own[k, rows, :] + part_in[k, rows, :]
            part_own[k, rows, :] = total
            part_half[k, rows, :] = total.astype(bf16)

        for d in near_first:
            back1b(k, d).start()
            back1c(k, d).start()

        @pl.when(k < N - 1)
        def _():
            back1a(k).start()

    def back2(g, src, d1, d2):
        return remote(src, in2.at[g, d2 * N + d1 - 1], r2s, r2r.at[g], peer(axes[g][0], d1, axes[g][1], d2))

    def block_of(ref, lead, row, xx):
        return ref.at[lead + (lanes(row + (xx // 2) * 16, 16, 16), lanes(lax.rem(xx, 2) * feat, feat, feat))]

    def sums_bc(k):
        await_all(elements(96, 2 * wide), r1r.at[k])
        total_b = part_own[k, lanes(128 + x_hi * 64, 64, 64), lanes(x_lo * feat, feat, feat)]
        total_c = part_own[k, lanes(256 + y * 32, 32, 32), :]
        for d in range(3):
            total_b += in1b[k, d].astype(f32)
            total_c += in1c[k, d].astype(f32)
        send2b[k] = total_b.astype(bf16)
        send2c[k] = total_c.astype(bf16)
        return total_b, total_c

    def send_bc(k, d1, r):
        back2(1, send2b.at[k, lanes(wrap(y + d1) * 16, 16, 16)], d1, r).start()
        back2(2, block_of(send2c, (k,), 0, wrap(x + d1)), d1, r).start()

    @pl.loop(0, N - 1)
    def _(k):
        sums_bc(k)
        for d1 in (2, 1, 3, 0):
            send_bc(k, d1, turn_back(k))

    await_all(in1a, r1ar)

    @pl.loop(0, N)
    def _(i):
        rows = pl.ds(pl.multiple_of(i * 32, 32), 32)
        total = part_own[N - 1, rows, :]
        for d in range(3):
            total += in1a[d, rows, :].astype(f32)
        send2a[rows, :] = total.astype(bf16)

        @pl.when(i == y)
        def _():
            mid_a[...] = total

    for d2 in (2, 1, 3, 0):
        for d1 in (2, 1, 3, 0):
            if d1 or d2:
                back2(0, block_of(send2a, (), wrap(y + d2) * 32, wrap(x + d1)), d1, d2).start()

    total_b, total_c = sums_bc(N - 1)
    mid_b[...] = total_b
    mid_c[...] = total_c
    for d1 in (2, 1, 3):
        send_bc(N - 1, d1, 0)

    sub8 = lax.broadcasted_iota(jnp.int32, (8, 128), 0)
    lane8 = lax.broadcasted_iota(jnp.int32, (8, 128), 1)
    lse_p, extra = stat_fin[0], stat_fin[1]
    mean_gap8, hit8 = jnp.roll(lse_p, -3, axis=0), jnp.roll(extra, -3, axis=0)
    losses = mask_row[...] * (lse_p - hit8 + divergence_weight * (mean_gap8 - lse_p + extra))
    lined = jnp.zeros((8, 128), f32)
    for g in range(3):
        at = row_of[g] - g * 128
        moved = pltpu.roll(losses, lax.rem(128 - at + g * 16, 128), 1)
        line = jnp.broadcast_to(moved[g : g + 1, :], (8, 128))
        lined = jnp.where((lane8 >= g * 16) & (lane8 < g * 16 + 16), line, lined)
    second = pltpu.roll(lined, 128 - 24, 1)
    loss_out[...] = jnp.where(sub8 == 0, lined, second)[0:2, 0:24]

    done = [None] * 3
    for g in (0, 1, 2):
        await_all(in2.at[g], r2r.at[g])
        if g == 1:
            total = mid_b[lanes(y * 16, 16, 16), :]
        else:
            total = (mid_a if g == 0 else mid_c)[lanes(x_hi * 16, 16, 16), lanes(x_lo * feat, feat, feat)]
        for i in range(15):
            total += in2[g, i].astype(f32)
        done[g] = total
    grad_out[...] = jnp.concatenate(done, axis=0).reshape(2, 24, feat).astype(bf16)

    await_all(elements(240, feat, 3), gas)
    await_all(elements(192, 2 * wide, 3), g3s)
    await_all(elements(384, 2 * wide, 2), gts)
    to_twin.wait_send()
    await_all(stat_in, as_)
    fin.wait_send()
    part_copy(2).wait_send()
    part_copy(3).wait_send()
    await_all(elements(192, 2 * wide, 3), r1s)
    await_all(in2, r2s)


def body(hidden, policy_head, frozen_head, targets, loss_mask):
    vocab = policy_head.shape[0]
    feat = hidden.shape[2]
    wide = 2 * feat
    f32, bf16 = jnp.float32, jnp.bfloat16
    V, D = pltpu.VMEM, pltpu.SemaphoreType.DMA
    scratch = [
        V((N, vocab, 2 * wide), bf16), V((N, vocab, 2 * wide), bf16), V((N, 384, 2 * wide), bf16),
        V((384, vocab), f32), V((384, vocab), f32), V((384, vocab), bf16),
        V((8, 256), f32), V((384, 128), f32), V((384, 128), f32), V((8, 128), f32), V((384, 128), f32), V((384, 128), f32),
        V((384, 128), f32), V((2, 8, 128), f32), V((8, 128), f32), V((8, 128), f32), V((63, 8, 128), f32), V((2, 8, 128), f32),
        V((N, 384, wide), f32), V((2, 384, wide), f32), V((N, 384, wide), f32), V((N, 384, wide), bf16),
        V((3, 128, wide), bf16), V((N, 3, 64, feat), bf16), V((N, 3, 32, wide), bf16),
        V((32, wide), f32), V((64, feat), f32), V((32, wide), f32),
        V((128, wide), bf16), V((N, 64, feat), bf16), V((N, 32, wide), bf16), V((3, 15, 16, feat), bf16),
        D((2, N)), D, D((3, N)), D, D((N,)), D, D((N,)),
        D((1,)), D((1,)), D, D, D((1,)), D((1,)),
        D((2,)), D((N,)), D, D, D((N,)), D, D((3,)),
        pltpu.SemaphoreType.REGULAR,
        D((3,)), V(hidden.shape, bf16), V(targets.shape, jnp.int32), V(loss_mask.shape, jnp.int32),
    ]
    vmem = pl.BlockSpec(memory_space=pltpu.VMEM)
    anywhere = pl.BlockSpec(memory_space=pl.ANY)
    results = pl.pallas_call(
        functools.partial(kernel, feat, vocab),
        out_shape=(
            jax.ShapeDtypeStruct(hidden.shape, bf16),
            jax.ShapeDtypeStruct(hidden.shape[:2], f32),
        ),
        in_specs=[anywhere] * 5,
        out_specs=(vmem, vmem),
        scratch_shapes=scratch,
        compiler_params=pltpu.CompilerParams(
            collective_id=0, has_side_effects=True, vmem_limit_bytes=63 * 2**20
        ),
    )(hidden, policy_head, frozen_head, targets, loss_mask)

    def hand_over(grad_in, loss_in, grad, loss):
        grad[...] = grad_in[...]
        loss[...] = loss_in[...]

    return pl.pallas_call(
        hand_over,
        out_shape=[jax.ShapeDtypeStruct(r.shape, r.dtype) for r in results],
        in_specs=[vmem, vmem],
        out_specs=[vmem, vmem],
    )(*results)


def solution(mesh):
    in_specs = (
        P(None, "section", "tensor"),
        P(("section", "tensor"), None),
        P(("section", "tensor"), None),
        P(),
        P(),
    )
    out_specs = (P(None, "section", "tensor"), P(None, "section"))
    return jax.shard_map(body, mesh=mesh, in_specs=in_specs, out_specs=out_specs, check_vma=False)
```

```python
import functools

import jax
import jax.numpy as jnp
from jax import lax
from jax.experimental import pallas as pl
from jax.experimental.pallas import tpu as pltpu
from jax.sharding import PartitionSpec as P

MESH = pl.DeviceIdType.MESH
divergence_weight = 0.1
gradient_scale = 32.0
N = 4
M = 192


def device(x, y, z, core):
    return {"section": (x // 2) * N + y, "tensor": (x % 2) * (2 * N) + z * 2 + core}


def wrap(a):
    return lax.rem(a, N)


def kernel(feat, vocab, hidden_in, policy, frozen, targets_in, mask_in, grad_out, loss_out,
           heads_p, heads_f, rows_all, tails, acc_p, acc_f, logit_grad,
           ints, target_col, mask_col, mask_row, lse_col, gap_col, stat_col, stat_loc, stat_twin, stat_chip, stat_in, stat_fin,
           part_own, part_send, part_in, part_half,
           in1a, in1b, in1c, mid_a, mid_b, mid_c, send2a, send2b, send2c, in2,
           head_sem, gas, gar, g3s, g3r, gts, gtr,
           ss, sr, as_, ar, fs, fr,
           ts, tr, r1s, r1ar, r1r, r2s, r2r, vouch_sem,
           small_sem, hidden, targets, loss_mask):
    f32, bf16 = jnp.float32, jnp.bfloat16
    section, tensor = lax.axis_index("section"), lax.axis_index("tensor")
    x_hi, y = section // N, wrap(section)
    x_lo, z, core = tensor // (2 * N), wrap(tensor // 2), lax.rem(tensor, 2)
    x = x_hi * 2 + x_lo
    twin = 1 - core
    here = {"x": x, "y": y, "z": z}
    fh = feat // 2
    wide = 2 * feat

    def peer(axis, d, axis2="x", d2=0):
        at = dict(here)
        at[axis] = wrap(at[axis] + d)
        at[axis2] = wrap(at[axis2] + d2)
        return device(at["x"], at["y"], at["z"], core)

    twin_id = device(x, y, z, twin)

    def lanes(start, size, unit):
        return pl.ds(pl.multiple_of(start, unit), size)

    def remote(src, dst, send, recv, to):
        return pltpu.make_async_remote_copy(src, dst, send, recv, device_id=to, device_id_type=MESH)

    def await_all(ref, sem):
        pltpu.make_async_copy(ref, ref, sem).wait()

    def elements(deep, groups, cols=2 * wide, both=1):
        return rows_all.at[pl.ds(0, deep), pl.ds(0, both), pl.ds(0, groups), 0, :, pl.ds(0, cols)]

    small = [pltpu.make_async_copy(src, dst, small_sem.at[i])
             for i, (src, dst) in enumerate(((hidden_in, hidden), (targets_in, targets), (mask_in, loss_mask)))]
    for copy in small:
        copy.start()

    def head_copy(head, held, which, k, zz):
        for cc in range(2):
            for half in range(2):
                for lo in range(2):
                    pltpu.make_async_copy(
                        head.at[:, lanes((lo * 2 * N + zz * 2 + cc) * feat + half * fh, fh, fh)],
                        held.at[zz, :, pl.ds(cc * wide + half * feat + lo * fh, fh)],
                        head_sem.at[which, k],
                    ).start()

    def head_wait(head, held, which, k, zz):
        pltpu.make_async_copy(head.at[:, pl.ds(0, 4 * feat)], held.at[zz], head_sem.at[which, k]).wait()

    def turn(k):
        return k ^ (k // 2)

    @pl.loop(0, N)
    def _(k):
        zz = wrap(z + turn(k))
        head_copy(policy, heads_p, 0, k, zz)
        head_copy(frozen, heads_f, 1, k, zz)

    barrier = pltpu.get_barrier_semaphore()
    for axis in "xyz":
        for d in range(1, N):
            pl.semaphore_signal(barrier, inc=1, device_id=peer(axis, d), device_id_type=MESH)
    pl.semaphore_signal(barrier, inc=1, device_id=twin_id, device_id_type=MESH)

    axes = (("x", "y", "z"), ("y", "z", "x"), ("x", "z", "y"))

    def piece1(g, p=slice(None)):
        if g == 2:
            return tails.at[z, p, y, x_hi, :, lanes(core * feat + x_lo * fh, fh, fh)]
        return rows_all.at[z, p, y, x_hi, :, lanes(core * wide + g * feat + x_lo * fh, fh, fh)]

    def piece2(g, axis, d):
        at = dict(here)
        at[axis] = wrap(at[axis] + d)
        if g == 0:
            return rows_all.at[at["z"], :, at["y"], :, :, lanes(core * wide, feat, feat)]
        if g == 1:
            return rows_all.at[at["z"], :, pl.ds(0, N), x_hi, :, lanes(core * wide + feat + x_lo * fh, fh, fh)]
        return tails.at[at["z"], :, at["y"], :, :, lanes(core * feat, feat, feat)]

    small[0].wait()
    for p in range(2):
        own = hidden[p].astype(f32)
        piece1(0, p)[...] = own[0:16, 0:fh].astype(bf16)
        piece1(1, p)[...] = own[0:16, fh:feat].astype(bf16)
        piece1(2, p)[...] = jnp.concatenate([own[16:24, 0:fh], own[16:24, fh:feat]], axis=0).astype(bf16)
    pl.semaphore_wait(barrier, 3 * (N - 1) + 1)
    for axis in "xy":
        for d in range(1, N):
            pl.semaphore_signal(vouch_sem, inc=1, device_id=peer(axis, d), device_id_type=MESH)

    near_first = (1, 3, 2)

    def block_copy(g, d1, d2):
        ref = piece1(g)
        return remote(ref, ref, gas, gar.at[g, (N - d2) % N], peer(axes[g][0], d1, axes[g][1], d2))

    def piece_wait(g, q):
        if q == 0:
            await_all(elements(1, 1, 3 * feat), gar.at[g, 0])
        else:
            await_all(piece2(g, axes[g][1], q), gar.at[g, q])

    def piece_copy(g, d, q):
        ref = piece2(g, axes[g][1], q)
        return remote(ref, ref, g3s, g3r.at[N - d if g == 0 else q], peer(axes[g][2], d))

    def blocks_out(d1s, d2s):
        for d2 in d2s:
            for d1 in d1s:
                for g in (1, 2, 0):
                    block_copy(g, d1, d2).start()

    blocks_out(near_first, (0,))
    blocks_out((0,), near_first)
    pl.semaphore_wait(vouch_sem, 2 * (N - 1))
    blocks_out(near_first, near_first)

    acc_p[...] = jnp.zeros_like(acc_p)
    acc_f[...] = jnp.zeros_like(acc_f)
    stat_col[...] = jnp.zeros_like(stat_col)
    ints[...] = jnp.zeros_like(ints)
    small[1].wait()
    small[2].wait()
    ints[0:2, 0:M] = targets[...].astype(f32)
    ints[2:4, 0:M] = loss_mask[...].astype(f32)
    for base, col in ((0, target_col), (2, mask_col)):
        for p in range(2):
            for half in range(2):
                line = ints[base + p : base + p + 1, half * 128 : half * 128 + 128]
                upright = jnp.broadcast_to(line, (128, 128)).T
                for q in range(16 if half == 0 else 8):
                    s, h = divmod(half * 16 + q, 3)
                    hi, yy = divmod(s, N)
                    row = yy * 32 + hi * 16 + h * 8 if h < 2 else 128 + yy * 16 + hi * 8
                    col[p, row : row + 8, :] = upright[q * 8 : q * 8 + 8, :]
            col[p, M:256, :] = jnp.zeros((256 - M, 128), f32)
    for p in range(2):
        for j in range(2):
            mask_row[p, j : j + 1, :] = mask_col[p, j * 128 : j * 128 + 128, :].T[0:1, :]

    contract = (((1,), (1,)), ((), ()))

    def twin_out(r):
        zz = wrap(z + r)
        for ref in (rows_all.at[zz, :, pl.ds(0, N), :, :, lanes(core * wide, wide, wide)],
                    tails.at[zz, :, :, :, :, lanes(core * feat, feat, feat)]):
            remote(ref, ref, gts, gtr.at[r], twin_id).start()

    def class_in(r):
        zz = wrap(z + r)
        await_all(elements(1, 6, both=2), gtr.at[r])
        for p in range(2):
            stacked = tails[zz, p].astype(f32).reshape(8, 16, wide)
            for half in range(2):
                flat = stacked[:, half * 8 : half * 8 + 8, :].reshape(64, wide).astype(bf16)
                for cc in range(2):
                    at = cc * wide + half * feat
                    rows_all[zz, p, N : N + 2, :, :, at : at + feat] = (
                        flat[:, cc * feat : (cc + 1) * feat].reshape(2, 2, 16, feat)
                    )

    def add_logits(acc, head, zz):
        product = lax.dot_general(rows_all[zz].reshape(2 * M, 2 * wide), head[zz], contract, preferred_element_type=f32)
        acc[...] += product.reshape(2, M, vocab)

    for q in (0, 1, 3, 2):
        for g in (1, 2, 0):
            piece_wait(g, q)
            if g == 0:
                for d in (1, 3):
                    piece_copy(g, d, q).start()
            elif q != 2:
                for d in near_first:
                    piece_copy(g, d, q).start()
    for q in near_first + (0,):
        piece_copy(0, 2, q).start()
    await_all(elements(1, 6), g3r.at[0])
    twin_out(0)
    for g in (1, 2):
        for d in near_first:
            piece_copy(g, d, 2).start()
    class_in(0)

    @pl.loop(0, N)
    def _(k):
        zz = wrap(z + turn(k))
        head_wait(policy, heads_p, 0, k, zz)
        add_logits(acc_p, heads_p, zz)

        @pl.when(k < N - 1)
        def _():
            await_all(elements(2, 5), g3r.at[turn(k + 1)])
            twin_out(turn(k + 1))

        head_wait(frozen, heads_f, 1, k, zz)
        add_logits(acc_f, heads_f, zz)

        @pl.when(k < N - 1)
        def _():
            class_in(turn(k + 1))

    shard = section * (4 * N) + tensor
    first = (shard * vocab).astype(f32)
    block = 32
    lane = lax.broadcasted_iota(jnp.int32, (block, 128), 1)
    tiles = vocab // 128

    def picked(p, rows, v):
        return (lane + v * 128).astype(f32) == target_col[p, rows, :] - first

    def local_stats(p):
        @pl.loop(0, M // block)
        def _(i):
            rows = pl.ds(pl.multiple_of(i * block, block), block)
            lp = [acc_p[p, rows, v * 128 : v * 128 + 128] for v in range(tiles)]
            lf = [acc_f[p, rows, v * 128 : v * 128 + 128] for v in range(tiles)]
            top_p = jnp.max(functools.reduce(jnp.maximum, lp), axis=1, keepdims=True)
            top_f = jnp.max(functools.reduce(jnp.maximum, lf), axis=1, keepdims=True)
            ep = [jnp.exp(a - top_p) for a in lp]
            sum_p = jnp.sum(functools.reduce(jnp.add, ep), axis=1, keepdims=True)
            gaps = jnp.sum(functools.reduce(jnp.add, [e * (a - b) for e, a, b in zip(ep, lp, lf)]), axis=1, keepdims=True)
            sum_f = jnp.sum(functools.reduce(jnp.add, [jnp.exp(b - top_f) for b in lf]), axis=1, keepdims=True)
            hit = jnp.sum(
                functools.reduce(jnp.add, [jnp.where(picked(p, rows, v), lp[v], 0.0) for v in range(tiles)]),
                axis=1, keepdims=True,
            )
            stat_col[p, rows, :] = jnp.where(
                lane == 0, top_p + jnp.log(sum_p),
                jnp.where(lane == 1, gaps / sum_p, jnp.where(lane == 2, top_f + jnp.log(sum_f), hit)),
            )

        stat_loc[p] = jnp.zeros((2, 8, 128), f32)
        for j in range(2):
            upright = stat_col[p, j * 128 : j * 128 + 128, :].T
            for s in range(4):
                stat_loc[p, s // 2, (s % 2) * 2 + j : (s % 2) * 2 + j + 1, :] = upright[s : s + 1, :]

    first_core = core == 0

    def merge(parts):
        top = functools.reduce(jnp.maximum, parts)
        scaled = [jnp.exp(t - top) for t in parts]
        total = functools.reduce(jnp.add, scaled)
        moved = [jnp.where(first_core, jnp.roll(s, 2, axis=0), 1.0) for s in scaled]
        weighted = functools.reduce(jnp.add, [m * t for m, t in zip(moved, parts)])
        below = jnp.where(first_core, jnp.roll(total, 2, axis=0), 1.0)
        sub = lax.broadcasted_iota(jnp.int32, (8, 128), 0)
        return jnp.where(sub < 2, top + jnp.log(total), weighted / below)

    def stat_copy(p, k):
        to = device(wrap(x + k // 16), wrap(y + k // 4), wrap(z + k), core)
        return remote(stat_chip.at[p], stat_in.at[p, k - 1], as_.at[p], ar.at[p], to)

    def hops(k):
        return sum(min(d, N - d) for d in (k // 16, k // 4 % N, k % N))

    def to_twin(p):
        return remote(stat_loc.at[p, twin], stat_twin.at[p], ss.at[p], sr.at[p], twin_id)

    def stats_out(p):
        to_twin(p).start()
        to_twin(p).wait_recv()
        stat_chip[p] = merge([stat_loc[p, core], stat_twin[p]])
        for k in sorted(range(1, 64), key=hops, reverse=True):
            stat_copy(p, k).start()

    def final_copy(p, which):
        return remote(stat_fin.at[p, which], stat_fin.at[p, which], fs.at[p], fr.at[p], twin_id)

    def stats_in(p):
        await_all(stat_in.at[p], ar.at[p])
        stat_fin[p, core] = merge([stat_chip[p]] + [stat_in[p, k] for k in range(63)])
        final_copy(p, core).start()
        final_copy(p, twin).wait_recv()
        for j in range(2):
            rows = slice(j * 128, j * 128 + 128)
            lse_col[rows, :] = jnp.broadcast_to(stat_fin[p, 0, j : j + 1, :], (128, 128)).T
            gap_col[rows, :] = jnp.broadcast_to(stat_fin[p, 0, 2 + j : 3 + j, :], (128, 128)).T

        @pl.loop(0, M // block)
        def _(i):
            rows = pl.ds(pl.multiple_of(i * block, block), block)
            lse, mean_gap, weight = lse_col[rows, :], gap_col[rows, :], gradient_scale * mask_col[p, rows, :]
            for v in range(tiles):
                at = slice(v * 128, v * 128 + 128)
                lp, lf = acc_p[p, rows, at], acc_f[p, rows, at]
                probs = jnp.exp(lp - lse)
                hot = jnp.where(picked(p, rows, v), 1.0, 0.0)
                g = weight * (probs - hot + divergence_weight * probs * (lp - lf - mean_gap))
                logit_grad[p, rows, at] = g.astype(bf16)

    def turn_back(k):
        return turn(k) ^ 2

    def part_copy(p, k):
        return remote(part_send.at[k], part_in.at[p, k], ts.at[p, k], tr.at[p, k], twin_id)

    def back1a(p, k):
        r = turn_back(k)
        src = part_half.at[p, k, pl.ds(0, N), :, :, pl.ds(0, feat)]
        return remote(src, in1a.at[p, r - 1], r1s.at[p], r1ar.at[p], peer("z", r))

    def back1b(p, k, d):
        to = wrap(x + d)
        src = part_half.at[p, k, pl.ds(0, N), to // 2, :, lanes(feat + lax.rem(to, 2) * fh, fh, fh)]
        return remote(src, in1b.at[p, k, d - 1], r1s.at[p], r1r.at[p, k], peer("x", d))

    def back1c(p, k, d):
        to = wrap(y + d)
        src = part_half.at[p, k, N + to // 2, lax.rem(to, 2)]
        return remote(src, in1c.at[p, k, d - 1], r1s.at[p], r1r.at[p, k], peer("y", d))

    def part_dot(p, k, half):
        zz = wrap(z + turn_back(k))
        product = jnp.dot(logit_grad[p], heads_p[zz, :, lanes(half * wide, wide, wide)], preferred_element_type=f32)
        return product.reshape(6, 2, 16, wide)

    def gradient_out(p):
        def twin_half(k):
            part_send[k] = part_dot(p, k, twin)
            part_copy(p, k).start()

        twin_half(0)
        twin_half(1)

        @pl.loop(0, N)
        def _(k):
            part_own[p, k] = part_dot(p, k, core)

            @pl.when(k < N - 2)
            def _():
                twin_half(k + 2)

            part_copy(p, k).wait_recv()

            @pl.loop(0, 6)
            def _(i):
                total = part_own[p, k, i] + part_in[p, k, i]
                part_own[p, k, i] = total
                part_half[p, k, i] = total.astype(bf16)

            for d in near_first:
                back1b(p, k, d).start()
                back1c(p, k, d).start()

            @pl.when(k < N - 1)
            def _():
                back1a(p, k).start()

        for k in range(N):
            part_copy(p, k).wait_send()

    def back2(p, g, src, d1, d2):
        return remote(src, in2.at[p, g, d2 * N + d1 - 1], r2s.at[p], r2r.at[p, g], peer(axes[g][0], d1, axes[g][1], d2))

    def sums_bc(p, k):
        await_all(elements(1, 3), r1r.at[p, k])
        total_b = part_own[p, k, 0:N, x_hi, :, lanes(feat + x_lo * fh, fh, fh)]
        total_c = part_own[p, k, N + y // 2, lax.rem(y, 2)]
        for d in range(3):
            total_b += in1b[p, k, d].astype(f32)
            total_c += in1c[p, k, d].astype(f32)
        stacked = []
        for xx in range(N):
            rows, at = slice(xx // 2 * 8, xx // 2 * 8 + 8), xx % 2 * fh
            stacked.append(jnp.concatenate([total_c[rows, at : at + fh], total_c[rows, feat + at : feat + at + fh]], axis=0))
        send2b[p, k] = total_b.astype(bf16)
        for xx in range(N):
            send2c[p, k, xx] = stacked[xx].astype(bf16)
        return total_b, stacked

    def send_bc(p, k, d1, r):
        back2(p, 1, send2b.at[p, k, wrap(y + d1)], d1, r).start()
        back2(p, 2, send2c.at[p, k, wrap(x + d1)], d1, r).start()

    def second_out(p):
        @pl.loop(0, N - 1)
        def _(k):
            sums_bc(p, k)
            for d1 in (2, 1, 3, 0):
                send_bc(p, k, d1, turn_back(k))

        await_all(in1a.at[p], r1ar.at[p])

        @pl.loop(0, N)
        def _(i):
            total = part_own[p, N - 1, i, :, :, 0:feat]
            for d in range(3):
                total += in1a[p, d, i].astype(f32)
            send2a[p, i] = total.astype(bf16)

            @pl.when(i == y)
            def _():
                mid_a[p] = total

        for d2 in (2, 1, 3, 0):
            for d1 in (2, 1, 3, 0):
                if d1 or d2:
                    to = wrap(x + d1)
                    src = send2a.at[p, wrap(y + d2), to // 2, :, lanes(lax.rem(to, 2) * fh, fh, fh)]
                    back2(p, 0, src, d1, d2).start()

        total_b, stacked = sums_bc(p, N - 1)
        mid_b[p] = total_b
        for xx in range(N):
            mid_c[p, xx] = stacked[xx]
        for d1 in (2, 1, 3):
            send_bc(p, N - 1, d1, 0)

    def losses_out(p):
        lane8 = lax.broadcasted_iota(jnp.int32, (8, 128), 1)
        lse_p, extra = stat_fin[p, 0], stat_fin[p, 1]
        mean_gap8, hit8 = jnp.roll(lse_p, -2, axis=0), jnp.roll(extra, -2, axis=0)
        losses = mask_row[p] * (lse_p - hit8 + divergence_weight * (mean_gap8 - lse_p + extra))
        whole = pltpu.roll(losses, lax.rem(128 - (y * 32 + x_hi * 16), 128), 1)
        rest = pltpu.roll(losses, lax.rem(128 + 16 - (y * 16 + x_hi * 8), 128), 1)
        line = jnp.where(lane8[0:1] < 16, whole[0:1], rest[1:2])
        loss_out[p : p + 1, :] = line[:, 0:24]

    def gradient_in(p):
        done = []
        for g in range(3):
            await_all(in2.at[p, g], r2r.at[p, g])
            if g == 0:
                total = mid_a[p, x_hi, :, lanes(x_lo * fh, fh, fh)]
            else:
                total = mid_b[p, y] if g == 1 else mid_c[p, x]
            for i in range(15):
                total += in2[p, g, i].astype(f32)
            done.append(total)
        upper = jnp.concatenate([done[0], done[1]], axis=1)
        lower = jnp.concatenate([done[2][0:8], done[2][8:16]], axis=1)
        grad_out[p] = jnp.concatenate([upper, lower], axis=0).astype(bf16)

    local_stats(0)
    stats_out(0)
    local_stats(1)
    stats_out(1)
    stats_in(0)
    gradient_out(0)
    stats_in(1)
    gradient_out(1)
    second_out(0)
    losses_out(0)
    losses_out(1)
    second_out(1)
    gradient_in(0)
    gradient_in(1)

    await_all(elements(3, 5, 3 * feat), gas)
    await_all(elements(3, 6, both=2), g3s)
    await_all(elements(4, 6, both=2), gts)
    for p in range(2):
        to_twin(p).wait_send()
        await_all(stat_in.at[p], as_.at[p])
        final_copy(p, core).wait_send()
        await_all(elements(3, 6), r1s.at[p])
        await_all(in2.at[p], r2s.at[p])


def body(hidden, policy_head, frozen_head, targets, loss_mask):
    vocab = policy_head.shape[0]
    feat = hidden.shape[2]
    wide, fh = 2 * feat, feat // 2
    f32, bf16 = jnp.float32, jnp.bfloat16
    V, D = pltpu.VMEM, pltpu.SemaphoreType.DMA
    scratch = [
        V((N, vocab, 2 * wide), bf16), V((N, vocab, 2 * wide), bf16),
        V((N, 2, 6, 2, 16, 2 * wide), bf16), V((N, 2, N, 2, 16, wide), bf16),
        V((2, M, vocab), f32), V((2, M, vocab), f32), V((2, M, vocab), bf16),
        V((8, 256), f32), V((2, 256, 128), f32), V((2, 256, 128), f32), V((2, 8, 128), f32), V((256, 128), f32), V((256, 128), f32),
        V((2, 256, 128), f32), V((2, 2, 8, 128), f32), V((2, 8, 128), f32), V((2, 8, 128), f32), V((2, 63, 8, 128), f32),
        V((2, 2, 8, 128), f32),
        V((2, N, 6, 2, 16, wide), f32), V((N, 6, 2, 16, wide), f32), V((2, N, 6, 2, 16, wide), f32),
        V((2, N, 6, 2, 16, wide), bf16),
        V((2, 3, N, 2, 16, feat), bf16), V((2, N, 3, N, 16, fh), bf16), V((2, N, 3, 16, wide), bf16),
        V((2, 2, 16, feat), f32), V((2, N, 16, fh), f32), V((2, N, 16, fh), f32),
        V((2, N, 2, 16, feat), bf16), V((2, N, N, 16, fh), bf16), V((2, N, N, 16, fh), bf16), V((2, 3, 15, 16, fh), bf16),
        D((2, N)), D, D((3, N)), D, D((N,)), D, D((N,)),
        D((2,)), D((2,)), D((2,)), D((2,)), D((2,)), D((2,)),
        D((2, N)), D((2, N)), D((2,)), D((2,)), D((2, N)), D((2,)), D((2, 3)),
        pltpu.SemaphoreType.REGULAR,
        D((3,)), V(hidden.shape, bf16), V(targets.shape, jnp.int32), V(loss_mask.shape, jnp.int32),
    ]
    vmem = pl.BlockSpec(memory_space=pltpu.VMEM)
    anywhere = pl.BlockSpec(memory_space=pl.ANY)
    results = pl.pallas_call(
        functools.partial(kernel, feat, vocab),
        out_shape=(
            jax.ShapeDtypeStruct(hidden.shape, bf16),
            jax.ShapeDtypeStruct(hidden.shape[:2], f32),
        ),
        in_specs=[anywhere] * 5,
        out_specs=(vmem, vmem),
        scratch_shapes=scratch,
        compiler_params=pltpu.CompilerParams(
            collective_id=0, has_side_effects=True, vmem_limit_bytes=63 * 2**20
        ),
    )(hidden, policy_head, frozen_head, targets, loss_mask)

    def hand_over(grad_in, loss_in, grad, loss):
        grad[...] = grad_in[...]
        loss[...] = loss_in[...]

    return pl.pallas_call(
        hand_over,
        out_shape=[jax.ShapeDtypeStruct(r.shape, r.dtype) for r in results],
        in_specs=[vmem, vmem],
        out_specs=[vmem, vmem],
    )(*results)


def solution(mesh):
    in_specs = (
        P(None, "section", "tensor"),
        P(("section", "tensor"), None),
        P(("section", "tensor"), None),
        P(),
        P(),
    )
    out_specs = (P(None, "section", "tensor"), P(None, "section"))
    return jax.shard_map(body, mesh=mesh, in_specs=in_specs, out_specs=out_specs, check_vma=False)
```

```python
import functools

import jax
import jax.numpy as jnp
from jax import lax
from jax.experimental import pallas as pl
from jax.experimental.pallas import tpu as pltpu
from jax.sharding import PartitionSpec as P

MESH = pl.DeviceIdType.MESH
divergence_weight = 0.1
gradient_scale = 32.0
N = 4
M = 192


def device(x, y, z, core):
    return {"section": (x // 2) * N + y, "tensor": (x % 2) * (2 * N) + z * 2 + core}


def wrap(a):
    return lax.rem(a, N)


def kernel(feat, vocab, hidden_in, policy, frozen, targets_in, mask_in, grad_out, loss_out,
           heads_p, heads_f, rows_all, tails, acc_p, acc_f, logit_grad,
           ints, target_col, mask_col, mask_row, lse_col, gap_col, stat_col, stat_loc, stat_twin, stat_chip, stat_in, stat_fin,
           part_own, part_send, part_in, part_half,
           in1a, in1b, in1c, mid_a, mid_b, mid_c, send2a, send2b, send2c, in2,
           head_sem, gas, gar, g3s, g3r, gts, gtr,
           ss, sr, as_, ar, fs, fr,
           ts, tr, r1s, r1ar, r1r, r2s, r2r, vouch_sem,
           small_sem, hidden, targets, loss_mask):
    f32, bf16 = jnp.float32, jnp.bfloat16
    section, tensor = lax.axis_index("section"), lax.axis_index("tensor")
    x_hi, y = section // N, wrap(section)
    x_lo, z, core = tensor // (2 * N), wrap(tensor // 2), lax.rem(tensor, 2)
    x = x_hi * 2 + x_lo
    twin = 1 - core
    here = {"x": x, "y": y, "z": z}
    fh = feat // 2
    wide = 2 * feat

    def peer(axis, d, axis2="x", d2=0):
        at = dict(here)
        at[axis] = wrap(at[axis] + d)
        at[axis2] = wrap(at[axis2] + d2)
        return device(at["x"], at["y"], at["z"], core)

    twin_id = device(x, y, z, twin)

    def lanes(start, size, unit):
        return pl.ds(pl.multiple_of(start, unit), size)

    def remote(src, dst, send, recv, to):
        return pltpu.make_async_remote_copy(src, dst, send, recv, device_id=to, device_id_type=MESH)

    def await_all(ref, sem):
        pltpu.make_async_copy(ref, ref, sem).wait()

    def elements(deep, groups, cols=2 * wide, both=1):
        return rows_all.at[pl.ds(0, deep), pl.ds(0, both), pl.ds(0, groups), 0, :, pl.ds(0, cols)]

    small = [pltpu.make_async_copy(src, dst, small_sem.at[i])
             for i, (src, dst) in enumerate(((hidden_in, hidden), (targets_in, targets), (mask_in, loss_mask)))]
    for copy in small:
        copy.start()

    def head_copy(head, held, which, k, zz):
        for cc in range(2):
            for half in range(2):
                for lo in range(2):
                    pltpu.make_async_copy(
                        head.at[:, lanes((lo * 2 * N + zz * 2 + cc) * feat + half * fh, fh, fh)],
                        held.at[zz, :, pl.ds(cc * wide + half * feat + lo * fh, fh)],
                        head_sem.at[which, k],
                    ).start()

    def head_wait(head, held, which, k, zz):
        pltpu.make_async_copy(head.at[:, pl.ds(0, 4 * feat)], held.at[zz], head_sem.at[which, k]).wait()

    def turn(k):
        return k ^ (k // 2)

    @pl.loop(0, N)
    def _(k):
        zz = wrap(z + turn(k))
        head_copy(policy, heads_p, 0, k, zz)
        head_copy(frozen, heads_f, 1, k, zz)

    barrier = pltpu.get_barrier_semaphore()
    for axis in "xyz":
        for d in range(1, N):
            pl.semaphore_signal(barrier, inc=1, device_id=peer(axis, d), device_id_type=MESH)
    pl.semaphore_signal(barrier, inc=1, device_id=twin_id, device_id_type=MESH)

    axes = (("x", "y", "z"), ("y", "z", "x"), ("x", "z", "y"))

    def piece1(g, p=slice(None)):
        if g == 2:
            return tails.at[z, p, y, x_hi, :, lanes(core * feat + x_lo * fh, fh, fh)]
        return rows_all.at[z, p, y, x_hi, :, lanes(core * wide + g * feat + x_lo * fh, fh, fh)]

    def piece2(g, axis, d):
        at = dict(here)
        at[axis] = wrap(at[axis] + d)
        if g == 0:
            return rows_all.at[at["z"], :, at["y"], :, :, lanes(core * wide, feat, feat)]
        if g == 1:
            return rows_all.at[at["z"], :, pl.ds(0, N), x_hi, :, lanes(core * wide + feat + x_lo * fh, fh, fh)]
        return tails.at[at["z"], :, at["y"], :, :, lanes(core * feat, feat, feat)]

    small[0].wait()
    for p in range(2):
        own = hidden[p].astype(f32)
        piece1(0, p)[...] = own[0:16, 0:fh].astype(bf16)
        piece1(1, p)[...] = own[0:16, fh:feat].astype(bf16)
        piece1(2, p)[...] = jnp.concatenate([own[16:24, 0:fh], own[16:24, fh:feat]], axis=0).astype(bf16)
    pl.semaphore_wait(barrier, 3 * (N - 1) + 1)
    for axis in "xy":
        for d in range(1, N):
            pl.semaphore_signal(vouch_sem, inc=1, device_id=peer(axis, d), device_id_type=MESH)

    near_first = (1, 3, 2)

    def block_copy(g, d1, d2):
        ref = piece1(g)
        return remote(ref, ref, gas, gar.at[g, (N - d2) % N], peer(axes[g][0], d1, axes[g][1], d2))

    def piece_wait(g, q):
        if q == 0:
            await_all(elements(1, 1, 3 * feat), gar.at[g, 0])
        else:
            await_all(piece2(g, axes[g][1], q), gar.at[g, q])

    def piece_copy(g, d, q):
        ref = piece2(g, axes[g][1], q)
        return remote(ref, ref, g3s, g3r.at[N - d if g == 0 else q], peer(axes[g][2], d))

    def blocks_out(d1s, d2s):
        for d2 in d2s:
            for d1 in d1s:
                for g in (1, 2, 0):
                    block_copy(g, d1, d2).start()

    blocks_out(near_first, (0,))
    blocks_out((0,), near_first)
    pl.semaphore_wait(vouch_sem, 2 * (N - 1))
    blocks_out(near_first, near_first)

    acc_p[...] = jnp.zeros_like(acc_p)
    acc_f[...] = jnp.zeros_like(acc_f)
    stat_col[...] = jnp.zeros_like(stat_col)
    ints[...] = jnp.zeros_like(ints)
    small[1].wait()
    small[2].wait()
    ints[0:2, 0:M] = targets[...].astype(f32)
    ints[2:4, 0:M] = loss_mask[...].astype(f32)
    for base, col in ((0, target_col), (2, mask_col)):
        for p in range(2):
            for half in range(2):
                line = ints[base + p : base + p + 1, half * 128 : half * 128 + 128]
                upright = jnp.broadcast_to(line, (128, 128)).T
                for q in range(16 if half == 0 else 8):
                    s, h = divmod(half * 16 + q, 3)
                    hi, yy = divmod(s, N)
                    row = yy * 32 + hi * 16 + h * 8 if h < 2 else 128 + yy * 16 + hi * 8
                    col[p, row : row + 8, :] = upright[q * 8 : q * 8 + 8, :]
            col[p, M:256, :] = jnp.zeros((256 - M, 128), f32)
    for p in range(2):
        for j in range(2):
            mask_row[p, j : j + 1, :] = mask_col[p, j * 128 : j * 128 + 128, :].T[0:1, :]

    contract = (((1,), (1,)), ((), ()))

    def twin_out(r):
        zz = wrap(z + r)
        for ref in (rows_all.at[zz, :, pl.ds(0, N), :, :, lanes(core * wide, wide, wide)],
                    tails.at[zz, :, :, :, :, lanes(core * feat, feat, feat)]):
            remote(ref, ref, gts, gtr.at[r], twin_id).start()

    def class_in(r):
        zz = wrap(z + r)
        await_all(elements(1, 6, both=2), gtr.at[r])
        for p in range(2):
            stacked = tails[zz, p].astype(f32).reshape(8, 16, wide)
            for half in range(2):
                flat = stacked[:, half * 8 : half * 8 + 8, :].reshape(64, wide).astype(bf16)
                for cc in range(2):
                    at = cc * wide + half * feat
                    rows_all[zz, p, N : N + 2, :, :, at : at + feat] = (
                        flat[:, cc * feat : (cc + 1) * feat].reshape(2, 2, 16, feat)
                    )

    def add_logits(acc, head, zz):
        product = lax.dot_general(rows_all[zz].reshape(2 * M, 2 * wide), head[zz], contract, preferred_element_type=f32)
        acc[...] += product.reshape(2, M, vocab)

    for q in (0, 1, 3, 2):
        for g in (1, 2, 0):
            piece_wait(g, q)
            if g == 0:
                for d in (1, 3):
                    piece_copy(g, d, q).start()
            elif q != 2:
                for d in near_first:
                    piece_copy(g, d, q).start()
    for q in near_first + (0,):
        piece_copy(0, 2, q).start()
    await_all(elements(1, 6), g3r.at[0])
    twin_out(0)
    for g in (1, 2):
        for d in near_first:
            piece_copy(g, d, 2).start()
    class_in(0)

    @pl.loop(0, N)
    def _(k):
        zz = wrap(z + turn(k))
        head_wait(policy, heads_p, 0, k, zz)
        add_logits(acc_p, heads_p, zz)

        @pl.when(k < N - 1)
        def _():
            await_all(elements(2, 5), g3r.at[turn(k + 1)])
            twin_out(turn(k + 1))

        head_wait(frozen, heads_f, 1, k, zz)
        add_logits(acc_f, heads_f, zz)

        @pl.when(k < N - 1)
        def _():
            class_in(turn(k + 1))

    shard = section * (4 * N) + tensor
    first = (shard * vocab).astype(f32)
    block = 32
    lane = lax.broadcasted_iota(jnp.int32, (block, 128), 1)
    tiles = vocab // 128

    def picked(p, rows, v):
        return (lane + v * 128).astype(f32) == target_col[p, rows, :] - first

    def local_stats(p):
        @pl.loop(0, M // block)
        def _(i):
            rows = pl.ds(pl.multiple_of(i * block, block), block)
            lp = [acc_p[p, rows, v * 128 : v * 128 + 128] for v in range(tiles)]
            lf = [acc_f[p, rows, v * 128 : v * 128 + 128] for v in range(tiles)]
            top_p = jnp.max(functools.reduce(jnp.maximum, lp), axis=1, keepdims=True)
            top_f = jnp.max(functools.reduce(jnp.maximum, lf), axis=1, keepdims=True)
            ep = [jnp.exp(a - top_p) for a in lp]
            sum_p = jnp.sum(functools.reduce(jnp.add, ep), axis=1, keepdims=True)
            gaps = jnp.sum(functools.reduce(jnp.add, [e * (a - b) for e, a, b in zip(ep, lp, lf)]), axis=1, keepdims=True)
            sum_f = jnp.sum(functools.reduce(jnp.add, [jnp.exp(b - top_f) for b in lf]), axis=1, keepdims=True)
            hit = jnp.sum(
                functools.reduce(jnp.add, [jnp.where(picked(p, rows, v), lp[v], 0.0) for v in range(tiles)]),
                axis=1, keepdims=True,
            )
            stat_col[p, rows, :] = jnp.where(
                lane == 0, top_p + jnp.log(sum_p),
                jnp.where(lane == 1, gaps / sum_p, jnp.where(lane == 2, top_f + jnp.log(sum_f), hit)),
            )

        stat_loc[p] = jnp.zeros((2, 8, 128), f32)
        for j in range(2):
            upright = stat_col[p, j * 128 : j * 128 + 128, :].T
            for s in range(4):
                stat_loc[p, s // 2, (s % 2) * 2 + j : (s % 2) * 2 + j + 1, :] = upright[s : s + 1, :]

    first_core = core == 0

    def merge(parts):
        top = functools.reduce(jnp.maximum, parts)
        scaled = [jnp.exp(t - top) for t in parts]
        total = functools.reduce(jnp.add, scaled)
        moved = [jnp.where(first_core, jnp.roll(s, 2, axis=0), 1.0) for s in scaled]
        weighted = functools.reduce(jnp.add, [m * t for m, t in zip(moved, parts)])
        below = jnp.where(first_core, jnp.roll(total, 2, axis=0), 1.0)
        sub = lax.broadcasted_iota(jnp.int32, (8, 128), 0)
        return jnp.where(sub < 2, top + jnp.log(total), weighted / below)

    def stat_copy(p, k):
        to = device(wrap(x + k // 16), wrap(y + k // 4), wrap(z + k), core)
        return remote(stat_chip.at[p], stat_in.at[p, k - 1], as_.at[p], ar.at[p], to)

    def hops(k):
        return sum(min(d, N - d) for d in (k // 16, k // 4 % N, k % N))

    def to_twin(p):
        return remote(stat_loc.at[p, twin], stat_twin.at[p], ss.at[p], sr.at[p], twin_id)

    def stats_out(p):
        to_twin(p).start()
        to_twin(p).wait_recv()
        stat_chip[p] = merge([stat_loc[p, core], stat_twin[p]])
        for k in sorted(range(1, 64), key=hops, reverse=True):
            stat_copy(p, k).start()

    def final_copy(p, which):
        return remote(stat_fin.at[p, which], stat_fin.at[p, which], fs.at[p], fr.at[p], twin_id)

    def stats_in(p):
        await_all(stat_in.at[p], ar.at[p])
        stat_fin[p, core] = merge([stat_chip[p]] + [stat_in[p, k] for k in range(63)])
        final_copy(p, core).start()
        final_copy(p, twin).wait_recv()
        for j in range(2):
            rows = slice(j * 128, j * 128 + 128)
            lse_col[rows, :] = jnp.broadcast_to(stat_fin[p, 0, j : j + 1, :], (128, 128)).T
            gap_col[rows, :] = jnp.broadcast_to(stat_fin[p, 0, 2 + j : 3 + j, :], (128, 128)).T

        @pl.loop(0, M // block)
        def _(i):
            rows = pl.ds(pl.multiple_of(i * block, block), block)
            lse, mean_gap, weight = lse_col[rows, :], gap_col[rows, :], gradient_scale * mask_col[p, rows, :]
            for v in range(tiles):
                at = slice(v * 128, v * 128 + 128)
                lp, lf = acc_p[p, rows, at], acc_f[p, rows, at]
                probs = jnp.exp(lp - lse)
                hot = jnp.where(picked(p, rows, v), 1.0, 0.0)
                g = weight * (probs - hot + divergence_weight * probs * (lp - lf - mean_gap))
                logit_grad[p, rows, at] = g.astype(bf16)

    def turn_back(k):
        return turn(k) ^ 2

    def part_copy(p, k):
        return remote(part_send.at[k], part_in.at[p, k], ts.at[p, k], tr.at[p, k], twin_id)

    def back1a(p, k):
        r = turn_back(k)
        src = part_half.at[p, k, pl.ds(0, N), :, :, pl.ds(0, feat)]
        return remote(src, in1a.at[p, r - 1], r1s.at[p], r1ar.at[p], peer("z", r))

    def back1b(p, k, d):
        to = wrap(x + d)
        src = part_half.at[p, k, pl.ds(0, N), to // 2, :, lanes(feat + lax.rem(to, 2) * fh, fh, fh)]
        return remote(src, in1b.at[p, k, d - 1], r1s.at[p], r1r.at[p, k], peer("x", d))

    def back1c(p, k, d):
        to = wrap(y + d)
        src = part_half.at[p, k, N + to // 2, lax.rem(to, 2)]
        return remote(src, in1c.at[p, k, d - 1], r1s.at[p], r1r.at[p, k], peer("y", d))

    def part_dot(p, k, half):
        zz = wrap(z + turn_back(k))
        product = jnp.dot(logit_grad[p], heads_p[zz, :, lanes(half * wide, wide, wide)], preferred_element_type=f32)
        return product.reshape(6, 2, 16, wide)

    def gradient_out(p):
        def twin_half(k):
            part_send[k] = part_dot(p, k, twin).astype(bf16)
            part_copy(p, k).start()

        twin_half(0)
        twin_half(1)

        @pl.loop(0, N)
        def _(k):
            part_own[p, k] = part_dot(p, k, core)

            @pl.when(k < N - 2)
            def _():
                twin_half(k + 2)

            part_copy(p, k).wait_recv()

            @pl.loop(0, 6)
            def _(i):
                total = part_own[p, k, i] + part_in[p, k, i].astype(f32)
                part_own[p, k, i] = total
                part_half[p, k, i] = total.astype(bf16)

            @pl.when(k < N - 1)
            def _():
                back1a(p, k).start()

            for d in (2, 1, 3):
                back1b(p, k, d).start()
                back1c(p, k, d).start()

        for k in range(N):
            part_copy(p, k).wait_send()

    def back2(p, g, src, d1, d2):
        return remote(src, in2.at[p, g, d2 * N + d1 - 1], r2s.at[p], r2r.at[p, g], peer(axes[g][0], d1, axes[g][1], d2))

    def sums_bc(p, k):
        await_all(elements(1, 3), r1r.at[p, k])
        total_b = part_own[p, k, 0:N, x_hi, :, lanes(feat + x_lo * fh, fh, fh)]
        total_c = part_own[p, k, N + y // 2, lax.rem(y, 2)]
        for d in range(3):
            total_b += in1b[p, k, d].astype(f32)
            total_c += in1c[p, k, d].astype(f32)
        stacked = []
        for xx in range(N):
            rows, at = slice(xx // 2 * 8, xx // 2 * 8 + 8), xx % 2 * fh
            stacked.append(jnp.concatenate([total_c[rows, at : at + fh], total_c[rows, feat + at : feat + at + fh]], axis=0))
        send2b[p, k] = total_b.astype(bf16)
        for xx in range(N):
            send2c[p, k, xx] = stacked[xx].astype(bf16)
        return total_b, stacked

    def send_bc(p, k, d1, r):
        back2(p, 1, send2b.at[p, k, wrap(y + d1)], d1, r).start()
        back2(p, 2, send2c.at[p, k, wrap(x + d1)], d1, r).start()

    def second_out(p):
        @pl.loop(0, N - 1)
        def _(k):
            sums_bc(p, k)
            for d1 in (2, 1, 3, 0):
                send_bc(p, k, d1, turn_back(k))

        await_all(in1a.at[p], r1ar.at[p])

        @pl.loop(0, N)
        def _(i):
            total = part_own[p, N - 1, i, :, :, 0:feat]
            for d in range(3):
                total += in1a[p, d, i].astype(f32)
            send2a[p, i] = total.astype(bf16)

            @pl.when(i == y)
            def _():
                mid_a[p] = total

        for d2 in (2, 1, 3, 0):
            for d1 in (2, 1, 3, 0):
                if d1 or d2:
                    to = wrap(x + d1)
                    src = send2a.at[p, wrap(y + d2), to // 2, :, lanes(lax.rem(to, 2) * fh, fh, fh)]
                    back2(p, 0, src, d1, d2).start()

        total_b, stacked = sums_bc(p, N - 1)
        mid_b[p] = total_b
        for xx in range(N):
            mid_c[p, xx] = stacked[xx]
        for d1 in (2, 1, 3):
            send_bc(p, N - 1, d1, 0)

    def losses_out(p):
        lane8 = lax.broadcasted_iota(jnp.int32, (8, 128), 1)
        lse_p, extra = stat_fin[p, 0], stat_fin[p, 1]
        mean_gap8, hit8 = jnp.roll(lse_p, -2, axis=0), jnp.roll(extra, -2, axis=0)
        losses = mask_row[p] * (lse_p - hit8 + divergence_weight * (mean_gap8 - lse_p + extra))
        whole = pltpu.roll(losses, lax.rem(128 - (y * 32 + x_hi * 16), 128), 1)
        rest = pltpu.roll(losses, lax.rem(128 + 16 - (y * 16 + x_hi * 8), 128), 1)
        line = jnp.where(lane8[0:1] < 16, whole[0:1], rest[1:2])
        loss_out[p : p + 1, :] = line[:, 0:24]

    def gradient_in(p):
        done = []
        for g in range(3):
            await_all(in2.at[p, g], r2r.at[p, g])
            if g == 0:
                total = mid_a[p, x_hi, :, lanes(x_lo * fh, fh, fh)]
            else:
                total = mid_b[p, y] if g == 1 else mid_c[p, x]
            for i in range(15):
                total += in2[p, g, i].astype(f32)
            done.append(total)
        upper = jnp.concatenate([done[0], done[1]], axis=1)
        lower = jnp.concatenate([done[2][0:8], done[2][8:16]], axis=1)
        grad_out[p] = jnp.concatenate([upper, lower], axis=0).astype(bf16)

    local_stats(0)
    stats_out(0)
    local_stats(1)
    stats_out(1)
    stats_in(0)
    gradient_out(0)
    stats_in(1)
    gradient_out(1)
    second_out(0)
    losses_out(0)
    losses_out(1)
    second_out(1)
    gradient_in(0)
    gradient_in(1)

    await_all(elements(3, 5, 3 * feat), gas)
    await_all(elements(3, 6, both=2), g3s)
    await_all(elements(4, 6, both=2), gts)
    for p in range(2):
        to_twin(p).wait_send()
        await_all(stat_in.at[p], as_.at[p])
        final_copy(p, core).wait_send()
        await_all(elements(3, 6), r1s.at[p])
        await_all(in2.at[p], r2s.at[p])


def body(hidden, policy_head, frozen_head, targets, loss_mask):
    vocab = policy_head.shape[0]
    feat = hidden.shape[2]
    wide, fh = 2 * feat, feat // 2
    f32, bf16 = jnp.float32, jnp.bfloat16
    V, D = pltpu.VMEM, pltpu.SemaphoreType.DMA
    scratch = [
        V((N, vocab, 2 * wide), bf16), V((N, vocab, 2 * wide), bf16),
        V((N, 2, 6, 2, 16, 2 * wide), bf16), V((N, 2, N, 2, 16, wide), bf16),
        V((2, M, vocab), f32), V((2, M, vocab), f32), V((2, M, vocab), bf16),
        V((8, 256), f32), V((2, 256, 128), f32), V((2, 256, 128), f32), V((2, 8, 128), f32), V((256, 128), f32), V((256, 128), f32),
        V((2, 256, 128), f32), V((2, 2, 8, 128), f32), V((2, 8, 128), f32), V((2, 8, 128), f32), V((2, 63, 8, 128), f32),
        V((2, 2, 8, 128), f32),
        V((2, N, 6, 2, 16, wide), f32), V((N, 6, 2, 16, wide), bf16), V((2, N, 6, 2, 16, wide), bf16),
        V((2, N, 6, 2, 16, wide), bf16),
        V((2, 3, N, 2, 16, feat), bf16), V((2, N, 3, N, 16, fh), bf16), V((2, N, 3, 16, wide), bf16),
        V((2, 2, 16, feat), f32), V((2, N, 16, fh), f32), V((2, N, 16, fh), f32),
        V((2, N, 2, 16, feat), bf16), V((2, N, N, 16, fh), bf16), V((2, N, N, 16, fh), bf16), V((2, 3, 15, 16, fh), bf16),
        D((2, N)), D, D((3, N)), D, D((N,)), D, D((N,)),
        D((2,)), D((2,)), D((2,)), D((2,)), D((2,)), D((2,)),
        D((2, N)), D((2, N)), D((2,)), D((2,)), D((2, N)), D((2,)), D((2, 3)),
        pltpu.SemaphoreType.REGULAR,
        D((3,)), V(hidden.shape, bf16), V(targets.shape, jnp.int32), V(loss_mask.shape, jnp.int32),
    ]
    vmem = pl.BlockSpec(memory_space=pltpu.VMEM)
    anywhere = pl.BlockSpec(memory_space=pl.ANY)
    results = pl.pallas_call(
        functools.partial(kernel, feat, vocab),
        out_shape=(
            jax.ShapeDtypeStruct(hidden.shape, bf16),
            jax.ShapeDtypeStruct(hidden.shape[:2], f32),
        ),
        in_specs=[anywhere] * 5,
        out_specs=(vmem, vmem),
        scratch_shapes=scratch,
        compiler_params=pltpu.CompilerParams(
            collective_id=0, has_side_effects=True, vmem_limit_bytes=63 * 2**20
        ),
    )(hidden, policy_head, frozen_head, targets, loss_mask)

    def hand_over(grad_in, loss_in, grad, loss):
        grad[...] = grad_in[...]
        loss[...] = loss_in[...]

    return pl.pallas_call(
        hand_over,
        out_shape=[jax.ShapeDtypeStruct(r.shape, r.dtype) for r in results],
        in_specs=[vmem, vmem],
        out_specs=[vmem, vmem],
    )(*results)


def solution(mesh):
    in_specs = (
        P(None, "section", "tensor"),
        P(("section", "tensor"), None),
        P(("section", "tensor"), None),
        P(),
        P(),
    )
    out_specs = (P(None, "section", "tensor"), P(None, "section"))
    return jax.shard_map(body, mesh=mesh, in_specs=in_specs, out_specs=out_specs, check_vma=False)
```
